32 devices in a mesh: dp: 8 (over y, x, core), strip: 4 (over z).
Axes of the slice: x: 2, y: 2, z: 4, core: 2. Of those that a mesh axis runs over, the one named last changes fastest.
Arguments:
- latents: bfloat16 [8, 4, 320, 128], P('dp', 'strip'), may hold values from -6 to 6
- cotangent: bfloat16 [8, 4, 320, 128], P('dp', 'strip'), may hold values from -6 to 6
- weight: bfloat16 [320, 2880], P('strip'), may hold values from -0.109375 to 0.109375
- master: float32 [336, 2880], P('dp'), may hold values from -0.21875 to 0.21875
- first_moment: float32 [336, 2880], P('dp'), may hold values from -6 to 6
- second_moment: float32 [336, 2880], P('dp'), may hold values from 0.005 to 0.05
- owner_list: int32 [320], replicated, may hold values from 0 to 7, as said below
Outputs:
- output: bfloat16 [8, 4, 320, 128], P('dp', 'strip')
- grad_input: bfloat16 [8, 4, 320, 128], P('dp', 'strip')
- new_weight: bfloat16 [320, 2880], P('strip')
- new_master: float32 [336, 2880], P('dp')
- new_first: float32 [336, 2880], P('dp')
- new_second: float32 [336, 2880], P('dp')
The draws below stay inside these ranges and needn't reach their ends.
Inputs may be any that keep to these rules, and one draw needn't show every extreme that they name: `owner_list`: each of the 8 ranks owns at least one and at most 42 buckets, and some rank owns exactly 42.
All inputs are finite; a program needn't handle non-finite values.
Results may differ from the reference program's by a relative error of at most 0.0033.
Values may be sent and summed in bfloat16 or wider, within the bound.
A program may use at most 64 MiB of HBM per device.

```python
import math
import jax
import jax.numpy as jnp
from jax import lax

C = 320
WID = 128
IMAGES = 8
HEIGHT = 4
OWNERS = 8
CAP = 42


def draw_owner_list(key, part):
    key_rank = jax.random.fold_in(key, 11)
    key_pick = jax.random.fold_in(key, 12)
    key_order = jax.random.fold_in(key, 13)
    rank_list = jax.random.permutation(key_rank, OWNERS).astype(jnp.int32)
    bucket_order = jax.random.permutation(key_order, C).astype(jnp.int32)
    extra_count = C - CAP - (OWNERS - 1)
    picked = jax.random.permutation(key_pick, (OWNERS - 1) * (CAP - 2))[:extra_count].astype(jnp.int32)
    extra = rank_list[1 + picked // (CAP - 2)]
    leader = jnp.zeros((CAP,), jnp.int32) + rank_list[0]
    values = jnp.concatenate([leader, rank_list[1:], extra.astype(jnp.int32)])
    return jnp.zeros((C,), jnp.int32).at[bucket_order].set(values)


def raised(drawn, rng, source, target, shards_of, factor):
    def block_of(axis_at):
        return (jnp.arange(drawn.shape[axis_at]) // (drawn.shape[axis_at] // shards_of)).reshape((-1,) + (1,) * (drawn.ndim - 1 - axis_at))

    first = jax.random.permutation(rng, shards_of)[block_of(target)]
    second = (block_of(target) + shards_of // 2) % shards_of
    return jnp.where((block_of(source) == first) | (block_of(source) == second), factor * drawn, drawn)


def block_levels(stream_key, shape, cuts, smallest, top_value):
    def one(axis_at, shards_of):
        steps = jax.random.uniform(jax.random.fold_in(jax.random.fold_in(stream_key, 6), axis_at), (shards_of,), jnp.float32, smallest / len(cuts), top_value / len(cuts))
        return jnp.repeat(jnp.exp(steps), shape[axis_at] // shards_of).reshape((-1,) + (1,) * (len(shape) - axis_at - 1))

    factor_of = one(*cuts[0])
    for cut in cuts[1:]:
        factor_of = factor_of * one(*cut)
    return factor_of


def centred(own_key, extent, scale, reach, cuts=(), kind=jnp.bfloat16):
    array = jax.random.normal(own_key, extent, jnp.float32) * scale
    if len(cuts) > 0:
        array = block_levels(own_key, extent, cuts, -0.22, 0.18) * array
    return jnp.clip(array, min=-reach, max=reach).astype(kind)


def gaussian_with(rng, shape, scale, limit, shards, heavy, held_as=jnp.bfloat16):
    array = scale * jax.random.normal(rng, shape, jnp.float32)
    if shards:
        array = array * block_levels(rng, shape, shards, -0.22, 0.18)
    return jnp.clip(raised(array, jax.random.fold_in(rng, 3), *heavy), -limit, limit).astype(held_as)


def setup_inputs(seed: int = 0) -> dict:
    keys = jax.random.split(jax.random.key(seed), 8)
    latents = centred(keys[0], (IMAGES, HEIGHT, C, WID), 1.0, 6.0, ((0, 8), (1, 4)))
    cotangent = gaussian_with(keys[1], (IMAGES, HEIGHT, C, WID), 1.0, 6.0, ((0, 8), (1, 4)), (0, 2, 8, 2.0))
    weight = centred(keys[2], (C, 9 * C), (9 * C) ** -0.5, 0.109375, ((0, 4),))
    master = centred(keys[3], (OWNERS * CAP, 9 * C), 0.015, 0.21875, ((0, 8),), jnp.float32)
    first_moment = centred(keys[4], (OWNERS * CAP, 9 * C), 0.5, 6.0, ((0, 8),), jnp.float32)
    second_moment = jnp.clip(jnp.exp(math.log(0.05) - 2.3025851 * jax.random.uniform(keys[5], (OWNERS * CAP, 9 * C), jnp.float32) ** block_levels(keys[5], (OWNERS * CAP, 9 * C), ((0, 8),), -0.2, 0.2)), 0.005, 0.05)
    owner_list = draw_owner_list(jax.random.fold_in(keys[7], 71), 0)
    return dict(latents=latents, cotangent=cotangent, weight=weight, master=master, first_moment=first_moment, second_moment=second_moment, owner_list=owner_list)


beta_first = 0.9
beta_second = 0.999
learn_rate = 0.01
epsilon = 1e-08
bias_first = 1.0 - 0.9 ** 10
bias_second = 1.0 - 0.999 ** 10

def patches(padded, direction):
    widened = jnp.pad(padded, ((0, 0), (0, 0), (1, 1)))
    height = padded.shape[0] - 2
    across = padded.shape[2]
    pieces = []
    for row_step in (-1, 0, 1):
        for col_step in (-1, 0, 1):
            row_start = 1 + direction * row_step
            col_start = 1 + direction * col_step
            pieces.append(widened[row_start:row_start + height, :, col_start:col_start + across])
    return jnp.concatenate(pieces, axis=1)

def flipped(weight):
    channels = weight.shape[0]
    return weight.reshape(channels, 9, channels).transpose(2, 1, 0).reshape(channels, 9 * channels)

def slot_tables(owner_list, capacity):
    count = owner_list.shape[0]
    same_owner = owner_list[:, None] == owner_list[None, :]
    earlier = jnp.arange(count, dtype=jnp.int32)[None, :] < jnp.arange(count, dtype=jnp.int32)[:, None]
    within = lax.optimization_barrier(jnp.sum((same_owner & earlier).astype(jnp.int32), axis=1)).astype(jnp.int32)
    return (owner_list * capacity + within).astype(jnp.int32)

def adam_update(grads, master, first_moment, second_moment, filled):
    first_new = beta_first * first_moment + (1.0 - beta_first) * grads
    second_new = beta_second * second_moment + (1.0 - beta_second) * grads * grads
    update = learn_rate * (first_new / bias_first) / (jnp.sqrt(second_new / bias_second) + epsilon)
    keep = filled[:, None]
    return (jnp.where(keep, master - update, master), jnp.where(keep, first_new, first_moment), jnp.where(keep, second_new, second_moment))

def reference(latents, cotangent, weight, master, first_moment, second_moment, owner_list):
    weight_float = weight.astype(jnp.float32)
    flipped_float = flipped(weight).astype(jnp.float32)
    row_pad = ((1, 1), (0, 0), (0, 0))

    def image_step(grad_sum, pair):
        pixels, upstream = pair
        pixels_float = pixels.astype(jnp.float32)
        active = jax.nn.silu(pixels_float).astype(jnp.bfloat16)
        forward_cols = patches(jnp.pad(active, row_pad), 1).astype(jnp.float32)
        convolved = jnp.einsum('ok,hkw->how', weight_float, forward_cols)
        output = (pixels_float + convolved).astype(jnp.bfloat16)
        backward_cols = patches(jnp.pad(upstream, row_pad), -1).astype(jnp.float32)
        spread = jnp.einsum('ck,hkw->hcw', flipped_float, backward_cols)
        sigmoid_val = jax.nn.sigmoid(pixels_float)
        derivative = sigmoid_val * (1.0 + pixels_float * (1.0 - sigmoid_val))
        upstream_float = upstream.astype(jnp.float32)
        grad_input = (upstream_float + spread * derivative).astype(jnp.bfloat16)
        grad_sum = grad_sum + jnp.einsum('how,hkw->ok', upstream_float, forward_cols)
        return (grad_sum, (output, grad_input))
    summed, (output, grad_input) = lax.scan(image_step, jnp.zeros((C, 9 * C), jnp.float32), (latents, cotangent))
    gradient = summed / jnp.sqrt(jnp.float32(IMAGES * HEIGHT * WID))
    slot_ids = slot_tables(owner_list, CAP)
    matches = slot_ids[None, :] == jnp.arange(OWNERS * CAP, dtype=jnp.int32)[:, None]
    bucket = lax.optimization_barrier(jnp.sum(jnp.where(matches, jnp.arange(C, dtype=jnp.int32)[None, :], 0), axis=1)).astype(jnp.int32)
    filled = jnp.any(matches, axis=1)
    slot_grad = jnp.where(filled[:, None], gradient[bucket], 0.0)
    new_master, new_first, new_second = adam_update(slot_grad, master, first_moment, second_moment, filled)
    new_weight = new_master[slot_ids].astype(jnp.bfloat16)
    return (output, grad_input, new_weight, new_master, new_first, new_second)
```

```python
import functools
import math

import jax
import jax.numpy as jnp
from jax import lax
from jax.experimental import pallas as pl
from jax.experimental.pallas import tpu as pltpu
from jax.sharding import PartitionSpec as P

beta_first = 0.9
beta_second = 0.999
learn_rate = 0.01
epsilon = 1e-08
bias_first = 1.0 - 0.9**10
bias_second = 1.0 - 0.999**10

MESH = pl.DeviceIdType.MESH
bf16 = jnp.bfloat16
f32 = jnp.float32


def shifted(x, step, wid):
    if step == 0:
        return x
    lane = lax.broadcasted_iota(jnp.int32, x.shape, 1) % wid
    moved = pltpu.roll(x, (-step) % x.shape[1], 1)
    return jnp.where(lane == (wid - 1 if step > 0 else 0), 0.0, moved)


def fill_cols(x, out_ref, wid):
    chans, total = x.shape
    zero = jnp.zeros((chans, wid), bf16)
    for dw in (-1, 0, 1):
        moved = shifted(x, dw, wid).astype(bf16)
        padded = jnp.concatenate([zero, moved, zero], axis=1)
        for dh in (-1, 0, 1):
            tap = 3 * (dh + 1) + dw + 1
            out_ref[tap * chans : (tap + 1) * chans, :] = padded[:, (1 + dh) * wid : (1 + dh) * wid + total]


def kernel(
    dp, ns, cap, capp,
    lat_ref, cot_ref, w_ref, master_ref, first_ref, second_ref, own_col, own_row,
    out_ref, gin_ref, nw_ref, nm_ref, nf_ref, nsec_ref,
    act_all, cot_all, cotp, actq, actg, cotg, cols, qcols, z_scr, conv_s, conv_r, spread_s, spread_r,
    gq, gacc, pub, slot_scr,
    s_act, r_act, s_cot, r_cot, s_aq, r_aq, s_cp, r_cp, s_cv, r_cv, s_sp, r_sp, s_g, r_g, s_pub, r_pub, s_fw,
):
    d = lax.axis_index("dp")
    s = lax.axis_index("strip")
    chans, wid = lat_ref.shape[2], lat_ref.shape[3]
    part = chans // ns
    sibling = d + 1 - 2 * lax.rem(d, 2)
    mine = pl.ds(pl.multiple_of(s * part, part), part)

    def copy(src, dst, ss, rs, to):
        return pltpu.make_async_remote_copy(
            src_ref=src, dst_ref=dst, send_sem=ss, recv_sem=rs, device_id=to, device_id_type=MESH
        )

    def strip_peer(i):
        return lax.rem(s + i, ns)

    def dp_peer(i):
        return lax.rem(d + i, dp)

    barrier = pltpu.get_barrier_semaphore()
    for i in range(1, ns):
        pl.semaphore_signal(barrier, inc=1, device_id=(d, strip_peer(i)), device_id_type=MESH)

    def greet(i, c):
        pl.semaphore_signal(barrier, inc=1, device_id=(dp_peer(i), s), device_id_type=MESH)
        return c

    lax.fori_loop(1, dp, greet, 0)
    pix = lat_ref[0, 0].astype(f32)
    sig = 1.0 / (1.0 + jnp.exp(-pix))
    act_all[s] = (pix * sig).astype(bf16)
    cot_all[s] = cot_ref[0, 0]
    pl.semaphore_wait(barrier, ns - 1 + dp - 1)

    def act_copy(i, block):
        return copy(act_all.at[block], act_all.at[block], s_act.at[i], r_act.at[block], (d, strip_peer(i)))

    def cot_copy(i, block):
        return copy(cot_all.at[block], cot_all.at[block], s_cot.at[i], r_cot.at[block], (d, strip_peer(i)))

    for i in range(1, ns):
        cot_copy(i, s).start()
    for i in range(1, ns):
        act_copy(i, s).start()

    oc = own_col[...]
    orow = own_row[...]
    a0 = lax.broadcasted_iota(jnp.int32, (chans, chans), 0)
    a1 = lax.broadcasted_iota(jnp.int32, (chans, chans), 1)
    same = oc == orow
    within_row = jnp.sum(jnp.where(same & (a0 < a1), 1.0, 0.0), axis=0, keepdims=True).astype(jnp.int32)
    within_col = jnp.sum(jnp.where(same & (a1 < a0), 1.0, 0.0), axis=1, keepdims=True).astype(jnp.int32)
    slot_row = orow * capp + within_row
    slot_scr[...] = oc * capp + within_col
    owned = jnp.sum(jnp.where(orow == d, 1.0, 0.0), axis=1, keepdims=True)
    keep = lax.broadcasted_iota(jnp.int32, (cap, 1), 0).astype(f32) < owned
    pick = jnp.where(
        lax.broadcasted_iota(jnp.int32, (dp * capp, chans), 0) == slot_row, 1.0, 0.0
    ).astype(bf16)

    for i in range(1, ns):
        cot_copy(i, strip_peer(i)).wait_recv()
    for row in range(ns):
        chosen = jnp.dot(pick, cot_all[row], preferred_element_type=f32).astype(bf16)
        cotp[:, :, row * wid : (row + 1) * wid] = chosen.reshape(dp, capp, wid)

    def cp_copy(j, block):
        return copy(cotp.at[j], cotg.at[block], s_cp.at[j], r_cp.at[block], (j, s))

    def send_cp(i, c):
        cp_copy(dp_peer(i), d).start()
        return c

    lax.fori_loop(1, dp, send_cp, 0)
    cotg[d] = cotp[d]

    for i in range(1, ns):
        act_copy(i, strip_peer(i)).wait_recv()
    for row in range(ns):
        actq[:, row * wid : (row + 1) * wid] = act_all[row, mine, :]

    def aq_copy(j, block):
        return copy(actq, actg.at[block], s_aq.at[j], r_aq.at[block], (j, s))

    def send_aq(i, c):
        aq_copy(dp_peer(i), d).start()
        return c

    lax.fori_loop(1, dp, send_aq, 0)
    actg[d] = actq[...]

    whole = jnp.concatenate([act_all[row] for row in range(ns)], axis=1).astype(f32)
    fill_cols(whole, cols, wid)
    conv = jnp.dot(w_ref[...], cols[...], preferred_element_type=f32)
    for row in range(ns):
        conv_s[row] = conv[:, row * wid : (row + 1) * wid].astype(bf16)

    def cv_copy(i, block):
        return copy(conv_s.at[strip_peer(i)], conv_r.at[block], s_cv.at[i], r_cv.at[block], (d, strip_peer(i)))

    upq = jnp.concatenate([cot_all[row, mine, :] for row in range(ns)], axis=1)
    z_scr[...] = lax.dot_general(w_ref[...], upq, (((0,), (0,)), ((), ())), preferred_element_type=f32)
    zero = jnp.zeros((chans, wid), f32)
    spread = None
    for dw in (-1, 0, 1):
        total = None
        for dh in (-1, 0, 1):
            tap = 3 * (dh + 1) + dw + 1
            piece = z_scr[tap * chans : (tap + 1) * chans, :]
            if dh == 1:
                piece = jnp.concatenate([zero, piece[:, : (ns - 1) * wid]], axis=1)
            if dh == -1:
                piece = jnp.concatenate([piece[:, wid:], zero], axis=1)
            total = piece if total is None else total + piece
        total = shifted(total, -dw, wid)
        spread = total if spread is None else spread + total
    for row in range(ns):
        spread_s[row] = spread[:, row * wid : (row + 1) * wid].astype(bf16)

    def sp_copy(i, block):
        return copy(spread_s.at[strip_peer(i)], spread_r.at[block], s_sp.at[i], r_sp.at[block], (d, strip_peer(i)))

    gacc[...] = jnp.zeros_like(gacc)

    def grad_of(j):
        fill_cols(actg[j].astype(f32), qcols, wid)
        gacc[...] += lax.dot_general(
            cotg[j], qcols[...], (((1,), (1,)), ((), ())), preferred_element_type=f32
        )

    grad_of(d)

    def grad_step(i, c):
        j = dp_peer(i)
        cp_copy(j, j).wait_recv()
        aq_copy(j, j).wait_recv()
        grad_of(j)
        return c

    lax.fori_loop(1, dp, grad_step, 0)
    gq[s] = (gacc[...] * (1.0 / math.sqrt(dp * ns * wid))).astype(bf16)

    def g_copy(i, block):
        return copy(gq.at[block], gq.at[block], s_g.at[i], r_g.at[block], (d, strip_peer(i)))

    for i in range(1, ns):
        g_copy(i, s).start()
    for i in range(1, ns):
        cv_copy(i, s).start()
        sp_copy(i, s).start()
    for i in range(1, ns):
        g_copy(i, strip_peer(i)).wait_recv()
    pieces = []
    for tap in range(9):
        for row in range(ns):
            pieces.append(gq[row, :, tap * part : (tap + 1) * part])
    grads = jnp.concatenate(pieces, axis=1).astype(f32)[:cap]
    first = first_ref[...]
    second = second_ref[...]
    master = master_ref[...]
    first_new = beta_first * first + (1.0 - beta_first) * grads
    second_new = beta_second * second + (1.0 - beta_second) * grads * grads
    update = learn_rate * (first_new / bias_first) / (jnp.sqrt(second_new / bias_second) + epsilon)
    master_new = jnp.where(keep, master - update, master)
    nm_ref[...] = master_new
    nf_ref[...] = jnp.where(keep, first_new, first)
    nsec_ref[...] = jnp.where(keep, second_new, second)
    pub[d] = jnp.concatenate(
        [master_new, jnp.zeros((capp - cap, master_new.shape[1]), f32)], axis=0
    ).astype(bf16)

    def pub_copy(i, j, block):
        return copy(pub.at[block], pub.at[block], s_pub.at[i], r_pub.at[block], (j, s))

    def fw_copy(block):
        return copy(pub.at[block], pub.at[block], s_fw.at[block], r_pub.at[block], (sibling, s))

    half = dp // 2

    def send_pub(i, c):
        pub_copy(i, dp_peer(2 * i), d).start()
        return c

    lax.fori_loop(1, half, send_pub, 0)
    fw_copy(d).start()

    for i in range(1, ns):
        cv_copy(i, strip_peer(i)).wait_recv()
        sp_copy(i, strip_peer(i)).wait_recv()
    conv_r[s] = conv_s[s]
    spread_r[s] = spread_s[s]
    pix = lat_ref[0, 0].astype(f32)
    sig = 1.0 / (1.0 + jnp.exp(-pix))
    out_ref[0, 0] = (pix + conv_r[...].reshape(chans, wid).astype(f32)).astype(bf16)
    back = spread_r[0].astype(f32)
    for row in range(1, ns):
        back = back + spread_r[row].astype(f32)
    gin_ref[0, 0] = (
        cot_ref[0, 0].astype(f32) + back * (sig * (1.0 + pix * (1.0 - sig)))
    ).astype(bf16)

    def forward(i, c):
        j = dp_peer(2 * i)
        pub_copy(i, j, j).wait_recv()
        fw_copy(j).start()
        return c

    lax.fori_loop(1, half, forward, 0)
    base = sibling

    def arrive(i, c):
        fw_copy(lax.rem(base + 2 * i, dp)).wait_recv()
        return c

    lax.fori_loop(0, half, arrive, 0)
    slots = slot_scr[mine, :]
    want = jnp.where(
        lax.broadcasted_iota(jnp.int32, (part, dp * capp), 1) == slots, 1.0, 0.0
    ).astype(bf16)
    nw_ref[...] = jnp.dot(
        want, pub[...].reshape(dp * capp, pub.shape[2]), preferred_element_type=f32
    ).astype(bf16)

    for i in range(1, ns):
        act_copy(i, s).wait_send()
        cot_copy(i, s).wait_send()
        cv_copy(i, s).wait_send()
        sp_copy(i, s).wait_send()
        g_copy(i, s).wait_send()

    def left(i, c):
        j = dp_peer(i)
        cp_copy(j, d).wait_send()
        aq_copy(j, d).wait_send()
        return c

    lax.fori_loop(1, dp, left, 0)

    def left_pub(i, c):
        pub_copy(i, dp_peer(2 * i), d).wait_send()
        fw_copy(dp_peer(2 * i)).wait_send()
        return c

    lax.fori_loop(1, half, left_pub, 0)
    fw_copy(d).wait_send()


def local(dp, ns, latents, cotangent, weight, master, first_moment, second_moment, owner_list):
    chans, wid = latents.shape[2], latents.shape[3]
    cap = master.shape[0]
    capp = -(-cap // 16) * 16
    part = chans // ns
    width = weight.shape[1]
    pixels = ns * wid
    dma = lambda n: pltpu.SemaphoreType.DMA((n,))
    vmem = pl.BlockSpec(memory_space=pltpu.VMEM)
    arrays = (latents, cotangent, weight, master, first_moment, second_moment)
    scratch = [
        pltpu.VMEM((ns, chans, wid), bf16),
        pltpu.VMEM((ns, chans, wid), bf16),
        pltpu.VMEM((dp, capp, pixels), bf16),
        pltpu.VMEM((part, pixels), bf16),
        pltpu.VMEM((dp, part, pixels), bf16),
        pltpu.VMEM((dp, capp, pixels), bf16),
        pltpu.VMEM((9 * chans, pixels), bf16),
        pltpu.VMEM((9 * part, pixels), bf16),
        pltpu.VMEM((9 * chans, pixels), f32),
        pltpu.VMEM((ns, part, wid), bf16),
        pltpu.VMEM((ns, part, wid), bf16),
        pltpu.VMEM((ns, chans, wid), bf16),
        pltpu.VMEM((ns, chans, wid), bf16),
        pltpu.VMEM((ns, capp, 9 * part), bf16),
        pltpu.VMEM((capp, 9 * part), f32),
        pltpu.VMEM((dp, capp, width), bf16),
        pltpu.VMEM((chans, 1), jnp.int32),
    ] + [dma(n) for n in (ns, ns, ns, ns, dp, dp, dp, dp, ns, ns, ns, ns, ns, ns, dp, dp, dp)]
    return tuple(
        pl.pallas_call(
            functools.partial(kernel, dp, ns, cap, capp),
            out_shape=[
                jax.ShapeDtypeStruct(a.shape, a.dtype)
                for a in (latents, cotangent, weight, master, first_moment, second_moment)
            ],
            in_specs=[vmem] * 8,
            out_specs=[vmem] * 6,
            scratch_shapes=scratch,
            compiler_params=pltpu.CompilerParams(
                collective_id=0, has_side_effects=True, vmem_limit_bytes=58 * 2**20
            ),
            cost_estimate=pl.CostEstimate(flops=10**9, bytes_accessed=6 * 10**6, transcendentals=10**5),
        )(*arrays, owner_list.reshape(chans, 1), owner_list.reshape(1, chans))
    )


def solution(mesh):
    image = P("dp", "strip", None, None)
    state = P("dp", None)
    in_specs = (image, image, P("strip", None), state, state, state, P())
    out_specs = (image, image, P("strip", None), state, state, state)
    fn = functools.partial(local, mesh.shape["dp"], mesh.shape["strip"])
    return jax.shard_map(fn, mesh=mesh, in_specs=in_specs, out_specs=out_specs, check_vma=False)
```

```python
import functools
import math

import jax
import jax.numpy as jnp
from jax import lax
from jax.experimental import pallas as pl
from jax.experimental.pallas import tpu as pltpu
from jax.sharding import PartitionSpec as P

beta_first = 0.9
beta_second = 0.999
learn_rate = 0.01
epsilon = 1e-08
bias_first = 1.0 - 0.9**10
bias_second = 1.0 - 0.999**10

MESH = pl.DeviceIdType.MESH
bf16 = jnp.bfloat16
f32 = jnp.float32


def shifted(x, step, wid):
    if step == 0:
        return x
    lane = lax.broadcasted_iota(jnp.int32, x.shape, 1) % wid
    moved = pltpu.roll(x, (-step) % x.shape[1], 1)
    return jnp.where(lane == (wid - 1 if step > 0 else 0), 0.0, moved)


def fill_cols(x, out_ref, wid):
    chans, total = x.shape
    zero = jnp.zeros((chans, wid), bf16)
    for dw in (-1, 0, 1):
        moved = shifted(x, dw, wid).astype(bf16)
        padded = jnp.concatenate([zero, moved, zero], axis=1)
        for dh in (-1, 0, 1):
            tap = 3 * (dh + 1) + dw + 1
            out_ref[tap * chans : (tap + 1) * chans, :] = padded[:, (1 + dh) * wid : (1 + dh) * wid + total]


def kernel(
    dp, ns, cap, capp,
    lat_ref, cot_ref, w_hbm, master_hbm, first_hbm, second_hbm, own_ref,
    out_ref, gin_ref, nw_ref, nm_hbm, nf_hbm, nsec_hbm,
    w_ref, master_ref, first_ref, second_ref, nm_ref, nf_ref, nsec_ref, actz,
    act_all, cot_all, cotp, actq, actg, cotg, cols, qcols, z_scr, conv_s, conv_r, spread_s, spread_r,
    gq, gacc, pub, slot_scr,
    s_act, r_act, s_cot, r_cot, s_aq, r_aq, s_cp, r_cp, s_cv, r_cv, s_sp, r_sp, s_g, r_g, s_pub, r_pub, s_fw, s_az, r_az, s_in, s_out,
):
    d = lax.axis_index("dp")
    s = lax.axis_index("strip")
    chans, wid = lat_ref.shape[2], lat_ref.shape[3]
    part = chans // ns
    sibling = d + 1 - 2 * lax.rem(d, 2)
    mine = pl.ds(pl.multiple_of(s * part, part), part)

    loads = [
        pltpu.make_async_copy(src, dst, s_in.at[k])
        for k, (src, dst) in enumerate(
            ((w_hbm, w_ref), (master_hbm, master_ref), (first_hbm, first_ref), (second_hbm, second_ref))
        )
    ]
    for load in loads:
        load.start()

    def copy(src, dst, ss, rs, to):
        return pltpu.make_async_remote_copy(
            src_ref=src, dst_ref=dst, send_sem=ss, recv_sem=rs, device_id=to, device_id_type=MESH
        )

    def strip_peer(i):
        return lax.rem(s + i, ns)

    def dp_peer(i):
        return lax.rem(d + i, dp)

    barrier = pltpu.get_barrier_semaphore()
    for i in range(1, ns):
        pl.semaphore_signal(barrier, inc=1, device_id=(d, strip_peer(i)), device_id_type=MESH)

    def greet(i, c):
        pl.semaphore_signal(barrier, inc=1, device_id=(dp_peer(i), s), device_id_type=MESH)
        return c

    lax.fori_loop(1, dp, greet, 0)
    pix = lat_ref[0, 0].astype(f32)
    sig = 1.0 / (1.0 + jnp.exp(-pix))
    act_all[s] = (pix * sig).astype(bf16)
    cot_all[s] = cot_ref[0, 0]
    actz[s] = act_all[s, mine, :]
    pl.semaphore_wait(barrier, ns - 1 + dp - 1)

    def act_copy(i, block):
        return copy(act_all.at[block], act_all.at[block], s_act.at[i], r_act.at[block], (d, strip_peer(i)))

    def cot_copy(i, block):
        return copy(cot_all.at[block], cot_all.at[block], s_cot.at[i], r_cot.at[block], (d, strip_peer(i)))

    for i in range(1, ns):
        cot_copy(i, s).start()
    def az_copy(i, block):
        rows = pl.ds(pl.multiple_of(strip_peer(i) * part, part), part)
        return copy(act_all.at[s, rows, :], actz.at[block], s_az.at[i], r_az.at[block], (d, strip_peer(i)))

    for i in range(1, ns):
        az_copy(i, s).start()

    orow = own_ref[...].reshape(1, chans)
    a0 = lax.broadcasted_iota(jnp.int32, (chans, chans), 0)
    a1 = lax.broadcasted_iota(jnp.int32, (chans, chans), 1)
    oc = jnp.sum(jnp.where(a0 == a1, orow.astype(f32), 0.0), axis=1, keepdims=True).astype(jnp.int32)
    same = oc == orow
    within_row = jnp.sum(jnp.where(same & (a0 < a1), 1.0, 0.0), axis=0, keepdims=True).astype(jnp.int32)
    within_col = jnp.sum(jnp.where(same & (a1 < a0), 1.0, 0.0), axis=1, keepdims=True).astype(jnp.int32)
    slot_row = orow * capp + within_row
    slot_scr[...] = oc * capp + within_col
    owned = jnp.sum(jnp.where(orow == d, 1.0, 0.0), axis=1, keepdims=True)
    keep = lax.broadcasted_iota(jnp.int32, (cap, 1), 0).astype(f32) < owned
    pick = jnp.where(
        lax.broadcasted_iota(jnp.int32, (dp * capp, chans), 0) == slot_row, 1.0, 0.0
    ).astype(bf16)

    for i in range(1, ns):
        cot_copy(i, strip_peer(i)).wait_recv()
    for row in range(ns):
        chosen = jnp.dot(pick, cot_all[row], preferred_element_type=f32).astype(bf16)
        cotp[:, :, row * wid : (row + 1) * wid] = chosen.reshape(dp, capp, wid)

    def cp_copy(j, block):
        return copy(cotp.at[j], cotg.at[block], s_cp.at[j], r_cp.at[block], (j, s))

    def send_cp(i, c):
        cp_copy(dp_peer(i), d).start()
        return c

    lax.fori_loop(1, dp, send_cp, 0)
    cotg[d] = cotp[d]

    for i in range(1, ns):
        az_copy(i, strip_peer(i)).wait_recv()
    for row in range(ns):
        actq[:, row * wid : (row + 1) * wid] = actz[row]

    def aq_copy(j, block):
        return copy(actq, actg.at[block], s_aq.at[j], r_aq.at[block], (j, s))

    def send_aq(i, c):
        aq_copy(dp_peer(i), d).start()
        return c

    lax.fori_loop(1, dp, send_aq, 0)
    actg[d] = actq[...]

    for i in range(1, ns):
        act_copy(i, s).start()

    loads[0].wait()
    upq = jnp.concatenate([cot_all[row, mine, :] for row in range(ns)], axis=1)
    z_scr[...] = lax.dot_general(w_ref[...], upq, (((0,), (0,)), ((), ())), preferred_element_type=f32)
    zero = jnp.zeros((chans, wid), f32)
    spread = None
    for dw in (-1, 0, 1):
        total = None
        for dh in (-1, 0, 1):
            tap = 3 * (dh + 1) + dw + 1
            piece = z_scr[tap * chans : (tap + 1) * chans, :]
            if dh == 1:
                piece = jnp.concatenate([zero, piece[:, : (ns - 1) * wid]], axis=1)
            if dh == -1:
                piece = jnp.concatenate([piece[:, wid:], zero], axis=1)
            total = piece if total is None else total + piece
        total = shifted(total, -dw, wid)
        spread = total if spread is None else spread + total
    for row in range(ns):
        spread_s[row] = spread[:, row * wid : (row + 1) * wid].astype(bf16)

    def sp_copy(i, block):
        return copy(spread_s.at[strip_peer(i)], spread_r.at[block], s_sp.at[i], r_sp.at[block], (d, strip_peer(i)))

    gacc[...] = jnp.zeros_like(gacc)

    def grad_of(j):
        fill_cols(actg[j].astype(f32), qcols, wid)
        gacc[...] += lax.dot_general(
            cotg[j], qcols[...], (((1,), (1,)), ((), ())), preferred_element_type=f32
        )

    grad_of(d)

    def grad_step(i, c):
        j = dp_peer(i)
        cp_copy(j, j).wait_recv()
        aq_copy(j, j).wait_recv()
        grad_of(j)
        return c

    lax.fori_loop(1, dp, grad_step, 0)
    gq[s] = (gacc[...] * (1.0 / math.sqrt(dp * ns * wid))).astype(bf16)

    def g_copy(i, block):
        return copy(gq.at[block], gq.at[block], s_g.at[i], r_g.at[block], (d, strip_peer(i)))

    for i in range(1, ns):
        g_copy(i, s).start()
    for i in range(1, ns):
        act_copy(i, strip_peer(i)).wait_recv()
    whole = jnp.concatenate([act_all[row] for row in range(ns)], axis=1).astype(f32)
    fill_cols(whole, cols, wid)
    conv = jnp.dot(w_ref[...], cols[...], preferred_element_type=f32)
    for row in range(ns):
        conv_s[row] = conv[:, row * wid : (row + 1) * wid].astype(bf16)

    def cv_copy(i, block):
        return copy(conv_s.at[strip_peer(i)], conv_r.at[block], s_cv.at[i], r_cv.at[block], (d, strip_peer(i)))

    for i in range(1, ns):
        g_copy(i, strip_peer(i)).wait_recv()
    for i in range(1, ns):
        cv_copy(i, s).start()
        sp_copy(i, s).start()
    for load in loads[1:]:
        load.wait()
    pieces = []
    for tap in range(9):
        for row in range(ns):
            pieces.append(gq[row, :, tap * part : (tap + 1) * part])
    grads = jnp.concatenate(pieces, axis=1).astype(f32)[:cap]
    first = first_ref[...]
    second = second_ref[...]
    master = master_ref[...]
    first_new = beta_first * first + (1.0 - beta_first) * grads
    second_new = beta_second * second + (1.0 - beta_second) * grads * grads
    update = learn_rate * (first_new / bias_first) / (jnp.sqrt(second_new / bias_second) + epsilon)
    master_new = jnp.where(keep, master - update, master)
    nm_ref[...] = master_new
    nf_ref[...] = jnp.where(keep, first_new, first)
    nsec_ref[...] = jnp.where(keep, second_new, second)
    pub[d] = jnp.concatenate(
        [master_new, jnp.zeros((capp - cap, master_new.shape[1]), f32)], axis=0
    ).astype(bf16)

    def pub_copy(i, j, block):
        return copy(pub.at[block], pub.at[block], s_pub.at[i], r_pub.at[block], (j, s))

    def fw_copy(block):
        return copy(pub.at[block], pub.at[block], s_fw.at[block], r_pub.at[block], (sibling, s))

    half = dp // 2

    def send_pub(i, c):
        pub_copy(i, dp_peer(2 * i), d).start()
        return c

    lax.fori_loop(1, half, send_pub, 0)
    fw_copy(d).start()
    stores = [
        pltpu.make_async_copy(src, dst, s_out.at[k])
        for k, (src, dst) in enumerate(((nm_ref, nm_hbm), (nf_ref, nf_hbm), (nsec_ref, nsec_hbm)))
    ]
    for store in stores:
        store.start()

    for i in range(1, ns):
        cv_copy(i, strip_peer(i)).wait_recv()
        sp_copy(i, strip_peer(i)).wait_recv()
    conv_r[s] = conv_s[s]
    spread_r[s] = spread_s[s]
    pix = lat_ref[0, 0].astype(f32)
    sig = 1.0 / (1.0 + jnp.exp(-pix))
    out_ref[0, 0] = (pix + conv_r[...].reshape(chans, wid).astype(f32)).astype(bf16)
    back = spread_r[0].astype(f32)
    for row in range(1, ns):
        back = back + spread_r[row].astype(f32)
    gin_ref[0, 0] = (
        cot_ref[0, 0].astype(f32) + back * (sig * (1.0 + pix * (1.0 - sig)))
    ).astype(bf16)

    def forward(i, c):
        j = dp_peer(2 * i)
        pub_copy(i, j, j).wait_recv()
        fw_copy(j).start()
        return c

    lax.fori_loop(1, half, forward, 0)
    base = sibling

    def arrive(i, c):
        fw_copy(lax.rem(base + 2 * i, dp)).wait_recv()
        return c

    lax.fori_loop(0, half, arrive, 0)
    slots = slot_scr[mine, :]
    want = jnp.where(
        lax.broadcasted_iota(jnp.int32, (part, dp * capp), 1) == slots, 1.0, 0.0
    ).astype(bf16)
    nw_ref[...] = jnp.dot(
        want, pub[...].reshape(dp * capp, pub.shape[2]), preferred_element_type=f32
    ).astype(bf16)

    for store in stores:
        store.wait()
    for i in range(1, ns):
        az_copy(i, s).wait_send()
        act_copy(i, s).wait_send()
        cot_copy(i, s).wait_send()
        cv_copy(i, s).wait_send()
        sp_copy(i, s).wait_send()
        g_copy(i, s).wait_send()

    def left(i, c):
        j = dp_peer(i)
        cp_copy(j, d).wait_send()
        aq_copy(j, d).wait_send()
        return c

    lax.fori_loop(1, dp, left, 0)

    def left_pub(i, c):
        pub_copy(i, dp_peer(2 * i), d).wait_send()
        fw_copy(dp_peer(2 * i)).wait_send()
        return c

    lax.fori_loop(1, half, left_pub, 0)
    fw_copy(d).wait_send()


def hand_over(*refs):
    sems = refs[12]
    copies = [pltpu.make_async_copy(refs[k], refs[6 + k], sems.at[k]) for k in range(6)]
    for c in copies:
        c.start()
    for c in copies:
        c.wait()


def local(dp, ns, latents, cotangent, weight, master, first_moment, second_moment, owner_list):
    chans, wid = latents.shape[2], latents.shape[3]
    cap = master.shape[0]
    capp = -(-cap // 16) * 16
    part = chans // ns
    width = weight.shape[1]
    pixels = ns * wid
    dma = lambda n: pltpu.SemaphoreType.DMA((n,))
    vmem = pl.BlockSpec(memory_space=pltpu.VMEM)
    arrays = (latents, cotangent, weight, master, first_moment, second_moment)
    anywhere = pl.BlockSpec(memory_space=pl.ANY)
    state = [pltpu.VMEM(master.shape, f32)] * 3
    scratch = [pltpu.VMEM(weight.shape, bf16)] + state + state + [
        pltpu.VMEM((ns, part, wid), bf16),
        pltpu.VMEM((ns, chans, wid), bf16),
        pltpu.VMEM((ns, chans, wid), bf16),
        pltpu.VMEM((dp, capp, pixels), bf16),
        pltpu.VMEM((part, pixels), bf16),
        pltpu.VMEM((dp, part, pixels), bf16),
        pltpu.VMEM((dp, capp, pixels), bf16),
        pltpu.VMEM((9 * chans, pixels), bf16),
        pltpu.VMEM((9 * part, pixels), bf16),
        pltpu.VMEM((9 * chans, pixels), f32),
        pltpu.VMEM((ns, part, wid), bf16),
        pltpu.VMEM((ns, part, wid), bf16),
        pltpu.VMEM((ns, chans, wid), bf16),
        pltpu.VMEM((ns, chans, wid), bf16),
        pltpu.VMEM((ns, capp, 9 * part), bf16),
        pltpu.VMEM((capp, 9 * part), f32),
        pltpu.VMEM((dp, capp, width), bf16),
        pltpu.VMEM((chans, 1), jnp.int32),
    ] + [dma(n) for n in (ns, ns, ns, ns, dp, dp, dp, dp, ns, ns, ns, ns, ns, ns, dp, dp, dp, ns, ns, 4, 3)]
    made = pl.pallas_call(
            functools.partial(kernel, dp, ns, cap, capp),
            out_shape=[
                jax.ShapeDtypeStruct(a.shape, a.dtype)
                for a in (latents, cotangent, weight, master, first_moment, second_moment)
            ],
            in_specs=[vmem] * 2 + [anywhere] * 4 + [vmem],
            out_specs=[vmem] * 3 + [anywhere] * 3,
            scratch_shapes=scratch,
            compiler_params=pltpu.CompilerParams(
                collective_id=0, has_side_effects=True, vmem_limit_bytes=58 * 2**20
            ),
            cost_estimate=pl.CostEstimate(flops=10**9, bytes_accessed=6 * 10**6, transcendentals=10**5),
        )(*arrays, owner_list)
    results = pl.pallas_call(
        hand_over,
        out_shape=[jax.ShapeDtypeStruct(a.shape, a.dtype) for a in arrays],
        in_specs=[anywhere] * 6,
        out_specs=[anywhere] * 6,
        scratch_shapes=[pltpu.SemaphoreType.DMA((6,))],
    )(*made)
    return tuple(results)


def solution(mesh):
    image = P("dp", "strip", None, None)
    state = P("dp", None)
    in_specs = (image, image, P("strip", None), state, state, state, P())
    out_specs = (image, image, P("strip", None), state, state, state)
    fn = functools.partial(local, mesh.shape["dp"], mesh.shape["strip"])
    return jax.shard_map(fn, mesh=mesh, in_specs=in_specs, out_specs=out_specs, check_vma=False)
```

```python
import functools
import math

import jax
import jax.numpy as jnp
from jax import lax
from jax.experimental import pallas as pl
from jax.experimental.pallas import tpu as pltpu
from jax.sharding import PartitionSpec as P

beta_first = 0.9
beta_second = 0.999
learn_rate = 0.01
epsilon = 1e-08
bias_first = 1.0 - 0.9**10
bias_second = 1.0 - 0.999**10

MESH = pl.DeviceIdType.MESH
bf16 = jnp.bfloat16
f32 = jnp.float32


def shifted(x, step, wid):
    if step == 0:
        return x
    lane = lax.broadcasted_iota(jnp.int32, x.shape, 1) % wid
    moved = pltpu.roll(x, (-step) % x.shape[1], 1)
    return jnp.where(lane == (wid - 1 if step > 0 else 0), 0.0, moved)


def fill_cols(x, out_ref, wid):
    chans, total = x.shape
    zero = jnp.zeros((chans, wid), bf16)
    for dw in (-1, 0, 1):
        moved = shifted(x, dw, wid).astype(bf16)
        padded = jnp.concatenate([zero, moved, zero], axis=1)
        for dh in (-1, 0, 1):
            tap = 3 * (dh + 1) + dw + 1
            out_ref[tap * chans : (tap + 1) * chans, :] = padded[:, (1 + dh) * wid : (1 + dh) * wid + total]


def kernel(
    dp, ns, cap, capp,
    lat_ref, cot_ref, w_hbm, master_hbm, first_hbm, second_hbm, own_ref,
    out_ref, gin_ref, nw_ref, nm_hbm, nf_hbm, nsec_hbm,
    w_ref, master_ref, first_ref, second_ref, nm_ref, nf_ref, nsec_ref, actz,
    act_all, cot_all, cotp, actq, actg, cotg, cols, qcols, z_scr, conv_s, conv_r, spread_s, spread_r,
    gq, gacc, pub, slot_scr,
    s_act, r_act, s_cot, r_cot, s_aq, r_aq, s_cp, r_cp, s_cv, r_cv, s_sp, r_sp, s_g, r_g, s_pub, r_pub, s_fw, s_az, r_az, s_in, s_out, s_aqf,
):
    d = lax.axis_index("dp")
    s = lax.axis_index("strip")
    chans, wid = lat_ref.shape[2], lat_ref.shape[3]
    part = chans // ns
    sibling = d + 1 - 2 * lax.rem(d, 2)
    mine = pl.ds(pl.multiple_of(s * part, part), part)

    loads = [
        pltpu.make_async_copy(src, dst, s_in.at[k])
        for k, (src, dst) in enumerate(
            ((w_hbm, w_ref), (master_hbm, master_ref), (first_hbm, first_ref), (second_hbm, second_ref))
        )
    ]
    for load in loads:
        load.start()

    def copy(src, dst, ss, rs, to):
        return pltpu.make_async_remote_copy(
            src_ref=src, dst_ref=dst, send_sem=ss, recv_sem=rs, device_id=to, device_id_type=MESH
        )

    def strip_peer(i):
        return lax.rem(s + i, ns)

    def dp_peer(i):
        return lax.rem(d + i, dp)

    barrier = pltpu.get_barrier_semaphore()
    for i in range(1, ns):
        pl.semaphore_signal(barrier, inc=1, device_id=(d, strip_peer(i)), device_id_type=MESH)

    def greet(i, c):
        pl.semaphore_signal(barrier, inc=1, device_id=(dp_peer(i), s), device_id_type=MESH)
        return c

    lax.fori_loop(1, dp, greet, 0)
    pix = lat_ref[0, 0].astype(f32)
    sig = 1.0 / (1.0 + jnp.exp(-pix))
    act_all[s] = (pix * sig).astype(bf16)
    cot_all[s] = cot_ref[0, 0]
    actz[s] = act_all[s, mine, :]
    pl.semaphore_wait(barrier, ns - 1 + dp - 1)

    def act_copy(i, block):
        return copy(act_all.at[block], act_all.at[block], s_act.at[i], r_act.at[block], (d, strip_peer(i)))

    def cot_copy(i, block):
        return copy(cot_all.at[block], cot_all.at[block], s_cot.at[i], r_cot.at[block], (d, strip_peer(i)))

    for i in range(1, ns):
        cot_copy(i, s).start()
    def az_copy(i, block):
        rows = pl.ds(pl.multiple_of(strip_peer(i) * part, part), part)
        return copy(act_all.at[s, rows, :], actz.at[block], s_az.at[i], r_az.at[block], (d, strip_peer(i)))

    for i in range(1, ns):
        az_copy(i, s).start()

    orow = own_ref[...].reshape(1, chans)
    a0 = lax.broadcasted_iota(jnp.int32, (chans, chans), 0)
    a1 = lax.broadcasted_iota(jnp.int32, (chans, chans), 1)
    oc = jnp.sum(jnp.where(a0 == a1, orow.astype(f32), 0.0), axis=1, keepdims=True).astype(jnp.int32)
    same = oc == orow
    within_row = jnp.sum(jnp.where(same & (a0 < a1), 1.0, 0.0), axis=0, keepdims=True).astype(jnp.int32)
    within_col = jnp.sum(jnp.where(same & (a1 < a0), 1.0, 0.0), axis=1, keepdims=True).astype(jnp.int32)
    slot_row = orow * capp + within_row
    slot_scr[...] = oc * capp + within_col
    owned = jnp.sum(jnp.where(orow == d, 1.0, 0.0), axis=1, keepdims=True)
    keep = lax.broadcasted_iota(jnp.int32, (cap, 1), 0).astype(f32) < owned
    pick = jnp.where(
        lax.broadcasted_iota(jnp.int32, (dp * capp, chans), 0) == slot_row, 1.0, 0.0
    ).astype(bf16)

    for i in range(1, ns):
        cot_copy(i, strip_peer(i)).wait_recv()
    for row in range(ns):
        chosen = jnp.dot(pick, cot_all[row], preferred_element_type=f32).astype(bf16)
        cotp[:, :, row * wid : (row + 1) * wid] = chosen.reshape(dp, capp, wid)

    def cp_copy(j, block):
        return copy(cotp.at[j], cotg.at[block], s_cp.at[j], r_cp.at[block], (j, s))

    def send_cp(i, c):
        cp_copy(dp_peer(i), d).start()
        return c

    lax.fori_loop(1, dp, send_cp, 0)
    cotg[d] = cotp[d]

    for i in range(1, ns):
        az_copy(i, strip_peer(i)).wait_recv()
    for row in range(ns):
        actq[:, row * wid : (row + 1) * wid] = actz[row]

    half = dp // 2

    def aq_copy(j, block):
        return copy(actg.at[block], actg.at[block], s_aq.at[j], r_aq.at[block], (j, s))

    def aqf_copy(block):
        return copy(actg.at[block], actg.at[block], s_aqf.at[block], r_aq.at[block], (sibling, s))

    def send_aq(i, c):
        aq_copy(dp_peer(2 * i), d).start()
        return c

    actg[d] = actq[...]
    lax.fori_loop(1, half, send_aq, 0)
    aqf_copy(d).start()

    for i in range(1, ns):
        act_copy(i, s).start()

    loads[0].wait()
    upq = jnp.concatenate([cot_all[row, mine, :] for row in range(ns)], axis=1)
    z_scr[...] = lax.dot_general(w_ref[...], upq, (((0,), (0,)), ((), ())), preferred_element_type=f32)
    zero = jnp.zeros((chans, wid), f32)
    spread = None
    for dw in (-1, 0, 1):
        total = None
        for dh in (-1, 0, 1):
            tap = 3 * (dh + 1) + dw + 1
            piece = z_scr[tap * chans : (tap + 1) * chans, :]
            if dh == 1:
                piece = jnp.concatenate([zero, piece[:, : (ns - 1) * wid]], axis=1)
            if dh == -1:
                piece = jnp.concatenate([piece[:, wid:], zero], axis=1)
            total = piece if total is None else total + piece
        total = shifted(total, -dw, wid)
        spread = total if spread is None else spread + total
    for row in range(ns):
        spread_s[row] = spread[:, row * wid : (row + 1) * wid].astype(bf16)

    def sp_copy(i, block):
        return copy(spread_s.at[strip_peer(i)], spread_r.at[block], s_sp.at[i], r_sp.at[block], (d, strip_peer(i)))

    gacc[...] = jnp.zeros_like(gacc)

    def grad_of(j):
        fill_cols(actg[j].astype(f32), qcols, wid)
        gacc[...] += lax.dot_general(
            qcols[...], cotg[j], (((1,), (1,)), ((), ())), preferred_element_type=f32
        )

    grad_of(d)

    def grad_near(i, c):
        j = dp_peer(2 * i)
        aq_copy(j, j).wait_recv()
        aqf_copy(j).start()
        cp_copy(j, j).wait_recv()
        grad_of(j)
        return c

    def grad_far(i, c):
        j = lax.rem(sibling + 2 * i, dp)
        aqf_copy(j).wait_recv()
        cp_copy(j, j).wait_recv()
        grad_of(j)
        return c

    lax.fori_loop(1, half, grad_near, 0)
    lax.fori_loop(0, half, grad_far, 0)
    gq[s] = (gacc[...].T * (1.0 / math.sqrt(dp * ns * wid))).astype(bf16)

    def g_copy(i, block):
        return copy(gq.at[block], gq.at[block], s_g.at[i], r_g.at[block], (d, strip_peer(i)))

    for i in range(1, ns):
        g_copy(i, s).start()
    for i in range(1, ns):
        act_copy(i, strip_peer(i)).wait_recv()
    whole = jnp.concatenate([act_all[row] for row in range(ns)], axis=1).astype(f32)
    fill_cols(whole, cols, wid)
    conv = jnp.dot(w_ref[...], cols[...], preferred_element_type=f32)
    for row in range(ns):
        conv_s[row] = conv[:, row * wid : (row + 1) * wid].astype(bf16)

    def cv_copy(i, block):
        return copy(conv_s.at[strip_peer(i)], conv_r.at[block], s_cv.at[i], r_cv.at[block], (d, strip_peer(i)))

    for i in range(1, ns):
        g_copy(i, strip_peer(i)).wait_recv()
    for i in range(1, ns):
        cv_copy(i, s).start()
        sp_copy(i, s).start()
    for load in loads[1:]:
        load.wait()
    pieces = []
    for tap in range(9):
        for row in range(ns):
            pieces.append(gq[row, :, tap * part : (tap + 1) * part])
    grads = jnp.concatenate(pieces, axis=1).astype(f32)[:cap]
    first = first_ref[...]
    second = second_ref[...]
    master = master_ref[...]
    first_new = beta_first * first + (1.0 - beta_first) * grads
    second_new = beta_second * second + (1.0 - beta_second) * grads * grads
    update = learn_rate * (first_new / bias_first) / (jnp.sqrt(second_new / bias_second) + epsilon)
    master_new = jnp.where(keep, master - update, master)
    nm_ref[...] = master_new
    nf_ref[...] = jnp.where(keep, first_new, first)
    nsec_ref[...] = jnp.where(keep, second_new, second)
    pub[d] = jnp.concatenate(
        [master_new, jnp.zeros((capp - cap, master_new.shape[1]), f32)], axis=0
    ).astype(bf16)

    def pub_copy(i, j, block):
        return copy(pub.at[block], pub.at[block], s_pub.at[i], r_pub.at[block], (j, s))

    def fw_copy(block):
        return copy(pub.at[block], pub.at[block], s_fw.at[block], r_pub.at[block], (sibling, s))

    def send_pub(i, c):
        pub_copy(i, dp_peer(2 * i), d).start()
        return c

    lax.fori_loop(1, half, send_pub, 0)
    fw_copy(d).start()
    stores = [
        pltpu.make_async_copy(src, dst, s_out.at[k])
        for k, (src, dst) in enumerate(((nm_ref, nm_hbm), (nf_ref, nf_hbm), (nsec_ref, nsec_hbm)))
    ]
    for store in stores:
        store.start()

    for i in range(1, ns):
        cv_copy(i, strip_peer(i)).wait_recv()
        sp_copy(i, strip_peer(i)).wait_recv()
    conv_r[s] = conv_s[s]
    spread_r[s] = spread_s[s]
    pix = lat_ref[0, 0].astype(f32)
    sig = 1.0 / (1.0 + jnp.exp(-pix))
    out_ref[0, 0] = (pix + conv_r[...].reshape(chans, wid).astype(f32)).astype(bf16)
    back = spread_r[0].astype(f32)
    for row in range(1, ns):
        back = back + spread_r[row].astype(f32)
    gin_ref[0, 0] = (
        cot_ref[0, 0].astype(f32) + back * (sig * (1.0 + pix * (1.0 - sig)))
    ).astype(bf16)

    def forward(i, c):
        j = dp_peer(2 * i)
        pub_copy(i, j, j).wait_recv()
        fw_copy(j).start()
        return c

    lax.fori_loop(1, half, forward, 0)
    base = sibling

    def arrive(i, c):
        fw_copy(lax.rem(base + 2 * i, dp)).wait_recv()
        return c

    lax.fori_loop(0, half, arrive, 0)
    slots = slot_scr[mine, :]
    want = jnp.where(
        lax.broadcasted_iota(jnp.int32, (part, dp * capp), 1) == slots, 1.0, 0.0
    ).astype(bf16)
    nw_ref[...] = jnp.dot(
        want, pub[...].reshape(dp * capp, pub.shape[2]), preferred_element_type=f32
    ).astype(bf16)

    for store in stores:
        store.wait()
    for i in range(1, ns):
        az_copy(i, s).wait_send()
        act_copy(i, s).wait_send()
        cot_copy(i, s).wait_send()
        cv_copy(i, s).wait_send()
        sp_copy(i, s).wait_send()
        g_copy(i, s).wait_send()

    def left(i, c):
        j = dp_peer(i)
        cp_copy(j, d).wait_send()
        return c

    lax.fori_loop(1, dp, left, 0)

    def left_pub(i, c):
        pub_copy(i, dp_peer(2 * i), d).wait_send()
        fw_copy(dp_peer(2 * i)).wait_send()
        aq_copy(dp_peer(2 * i), d).wait_send()
        aqf_copy(dp_peer(2 * i)).wait_send()
        return c

    lax.fori_loop(1, half, left_pub, 0)
    fw_copy(d).wait_send()
    aqf_copy(d).wait_send()


def hand_over(*refs):
    ins, outs, bufs, sem_in, sem_out = refs[:6], refs[6:12], refs[12:18], refs[18], refs[19]
    reads = [pltpu.make_async_copy(ins[k], bufs[k], sem_in.at[k]) for k in range(6)]
    writes = [pltpu.make_async_copy(bufs[k], outs[k], sem_out.at[k]) for k in range(6)]
    for c in reads:
        c.start()
    for k in range(6):
        reads[k].wait()
        writes[k].start()
    for c in writes:
        c.wait()


def local(dp, ns, latents, cotangent, weight, master, first_moment, second_moment, owner_list):
    chans, wid = latents.shape[2], latents.shape[3]
    cap = master.shape[0]
    capp = -(-cap // 16) * 16
    part = chans // ns
    width = weight.shape[1]
    pixels = ns * wid
    dma = lambda n: pltpu.SemaphoreType.DMA((n,))
    vmem = pl.BlockSpec(memory_space=pltpu.VMEM)
    arrays = (latents, cotangent, weight, master, first_moment, second_moment)
    anywhere = pl.BlockSpec(memory_space=pl.ANY)
    state = [pltpu.VMEM(master.shape, f32)] * 3
    scratch = [pltpu.VMEM(weight.shape, bf16)] + state + state + [
        pltpu.VMEM((ns, part, wid), bf16),
        pltpu.VMEM((ns, chans, wid), bf16),
        pltpu.VMEM((ns, chans, wid), bf16),
        pltpu.VMEM((dp, capp, pixels), bf16),
        pltpu.VMEM((part, pixels), bf16),
        pltpu.VMEM((dp, part, pixels), bf16),
        pltpu.VMEM((dp, capp, pixels), bf16),
        pltpu.VMEM((9 * chans, pixels), bf16),
        pltpu.VMEM((9 * part, pixels), bf16),
        pltpu.VMEM((9 * chans, pixels), f32),
        pltpu.VMEM((ns, part, wid), bf16),
        pltpu.VMEM((ns, part, wid), bf16),
        pltpu.VMEM((ns, chans, wid), bf16),
        pltpu.VMEM((ns, chans, wid), bf16),
        pltpu.VMEM((ns, capp, 9 * part), bf16),
        pltpu.VMEM((9 * part, capp), f32),
        pltpu.VMEM((dp, capp, width), bf16),
        pltpu.VMEM((chans, 1), jnp.int32),
    ] + [dma(n) for n in (ns, ns, ns, ns, dp, dp, dp, dp, ns, ns, ns, ns, ns, ns, dp, dp, dp, ns, ns, 4, 3, dp)]
    made = pl.pallas_call(
            functools.partial(kernel, dp, ns, cap, capp),
            out_shape=[
                jax.ShapeDtypeStruct(a.shape, a.dtype)
                for a in (latents, cotangent, weight, master, first_moment, second_moment)
            ],
            in_specs=[vmem] * 2 + [anywhere] * 4 + [vmem],
            out_specs=[vmem] * 3 + [anywhere] * 3,
            scratch_shapes=scratch,
            compiler_params=pltpu.CompilerParams(
                collective_id=0, has_side_effects=True, vmem_limit_bytes=58 * 2**20
            ),
            cost_estimate=pl.CostEstimate(flops=10**9, bytes_accessed=6 * 10**6, transcendentals=10**5),
        )(*arrays, owner_list)
    results = pl.pallas_call(
        hand_over,
        out_shape=[jax.ShapeDtypeStruct(a.shape, a.dtype) for a in arrays],
        in_specs=[anywhere] * 6,
        out_specs=[anywhere] * 6,
        scratch_shapes=[pltpu.VMEM(a.shape, a.dtype) for a in arrays] + [dma(6), dma(6)],
    )(*made)
    return tuple(results)


def solution(mesh):
    image = P("dp", "strip", None, None)
    state = P("dp", None)
    in_specs = (image, image, P("strip", None), state, state, state, P())
    out_specs = (image, image, P("strip", None), state, state, state)
    fn = functools.partial(local, mesh.shape["dp"], mesh.shape["strip"])
    return jax.shard_map(fn, mesh=mesh, in_specs=in_specs, out_specs=out_specs, check_vma=False)
```

```python
import functools
import math

import jax
import jax.numpy as jnp
from jax import lax
from jax.experimental import pallas as pl
from jax.experimental.pallas import tpu as pltpu
from jax.sharding import PartitionSpec as P

beta_first = 0.9
beta_second = 0.999
learn_rate = 0.01
epsilon = 1e-08
bias_first = 1.0 - 0.9**10
bias_second = 1.0 - 0.999**10

MESH = pl.DeviceIdType.MESH
bf16 = jnp.bfloat16
f32 = jnp.float32


def shifted(x, step, wid):
    if step == 0:
        return x
    lane = lax.broadcasted_iota(jnp.int32, x.shape, 1) % wid
    moved = pltpu.roll(x, (-step) % x.shape[1], 1)
    return jnp.where(lane == (wid - 1 if step > 0 else 0), 0.0, moved)


def fill_cols(x, out_ref, wid):
    chans, total = x.shape
    zero = jnp.zeros((chans, wid), bf16)
    for dw in (-1, 0, 1):
        moved = shifted(x, dw, wid).astype(bf16)
        padded = jnp.concatenate([zero, moved, zero], axis=1)
        for dh in (-1, 0, 1):
            tap = 3 * (dh + 1) + dw + 1
            out_ref[tap * chans : (tap + 1) * chans, :] = padded[:, (1 + dh) * wid : (1 + dh) * wid + total]


def kernel(
    dp, ns, cap, capp,
    lat_ref, cot_ref, w_hbm, master_hbm, first_hbm, second_hbm, own_ref,
    out_ref, gin_ref, nw_ref, nm_hbm, nf_hbm, nsec_hbm,
    w_ref, master_ref, first_ref, second_ref, nm_ref, nf_ref, nsec_ref, actz,
    act_all, cot_all, cotp, actq, actg, cotg, cols, qcols, z_scr, conv_s, conv_r, spread_s, spread_r,
    gq, gacc, pub, slot_scr, wacc,
    s_act, r_act, s_cot, r_cot, s_aq, r_aq, s_cp, r_cp, s_cv, r_cv, s_sp, r_sp, s_g, r_g, s_pub, r_pub, s_fw, s_az, r_az, s_in, s_out, s_aqf,
):
    d = lax.axis_index("dp")
    s = lax.axis_index("strip")
    chans, wid = lat_ref.shape[2], lat_ref.shape[3]
    part = chans // ns
    sibling = d + 1 - 2 * lax.rem(d, 2)
    mine = pl.ds(pl.multiple_of(s * part, part), part)

    loads = [
        pltpu.make_async_copy(src, dst, s_in.at[k])
        for k, (src, dst) in enumerate(
            ((w_hbm, w_ref), (master_hbm, master_ref), (first_hbm, first_ref), (second_hbm, second_ref))
        )
    ]
    for load in loads:
        load.start()

    def copy(src, dst, ss, rs, to):
        return pltpu.make_async_remote_copy(
            src_ref=src, dst_ref=dst, send_sem=ss, recv_sem=rs, device_id=to, device_id_type=MESH
        )

    def strip_peer(i):
        return lax.rem(s + i, ns)

    def dp_peer(i):
        return lax.rem(d + i, dp)

    barrier = pltpu.get_barrier_semaphore()
    for i in range(1, ns):
        pl.semaphore_signal(barrier, inc=1, device_id=(d, strip_peer(i)), device_id_type=MESH)

    def greet(i, c):
        pl.semaphore_signal(barrier, inc=1, device_id=(dp_peer(i), s), device_id_type=MESH)
        return c

    lax.fori_loop(1, dp, greet, 0)
    pix = lat_ref[0, 0].astype(f32)
    sig = 1.0 / (1.0 + jnp.exp(-pix))
    act_all[s] = (pix * sig).astype(bf16)
    cot_all[s] = cot_ref[0, 0]
    actz[s] = act_all[s, mine, :]
    pl.semaphore_wait(barrier, ns - 1 + dp - 1)

    def act_copy(i, block):
        return copy(act_all.at[block], act_all.at[block], s_act.at[i], r_act.at[block], (d, strip_peer(i)))

    def cot_copy(i, block):
        return copy(cot_all.at[block], cot_all.at[block], s_cot.at[i], r_cot.at[block], (d, strip_peer(i)))

    for i in range(1, ns):
        cot_copy(i, s).start()
    def az_copy(i, block):
        rows = pl.ds(pl.multiple_of(strip_peer(i) * part, part), part)
        return copy(act_all.at[s, rows, :], actz.at[block], s_az.at[i], r_az.at[block], (d, strip_peer(i)))

    for i in range(1, ns):
        az_copy(i, s).start()

    orow = own_ref[...].reshape(1, chans)
    a0 = lax.broadcasted_iota(jnp.int32, (chans, chans), 0)
    a1 = lax.broadcasted_iota(jnp.int32, (chans, chans), 1)
    oc = jnp.sum(jnp.where(a0 == a1, orow.astype(f32), 0.0), axis=1, keepdims=True).astype(jnp.int32)
    same = oc == orow
    within_row = jnp.sum(jnp.where(same & (a0 < a1), 1.0, 0.0), axis=0, keepdims=True).astype(jnp.int32)
    within_col = jnp.sum(jnp.where(same & (a1 < a0), 1.0, 0.0), axis=1, keepdims=True).astype(jnp.int32)
    slot_row = orow * capp + within_row
    slot_scr[...] = oc * capp + within_col
    owned = jnp.sum(jnp.where(orow == d, 1.0, 0.0), axis=1, keepdims=True)
    keep = lax.broadcasted_iota(jnp.int32, (cap, 1), 0).astype(f32) < owned
    pick = jnp.where(
        lax.broadcasted_iota(jnp.int32, (dp * capp, chans), 0) == slot_row, 1.0, 0.0
    ).astype(bf16)

    for i in range(1, ns):
        cot_copy(i, strip_peer(i)).wait_recv()
    for row in range(ns):
        chosen = jnp.dot(pick, cot_all[row], preferred_element_type=f32).astype(bf16)
        cotp[:, :, row * wid : (row + 1) * wid] = chosen.reshape(dp, capp, wid)

    def cp_copy(j, block):
        return copy(cotp.at[j], cotg.at[block], s_cp.at[j], r_cp.at[block], (j, s))

    def send_cp(i, c):
        cp_copy(dp_peer(i), d).start()
        return c

    lax.fori_loop(1, dp, send_cp, 0)
    cotg[d] = cotp[d]

    for i in range(1, ns):
        az_copy(i, strip_peer(i)).wait_recv()
    for row in range(ns):
        actq[:, row * wid : (row + 1) * wid] = actz[row]

    half = dp // 2

    def aq_copy(j, block):
        return copy(actg.at[block], actg.at[block], s_aq.at[j], r_aq.at[block], (j, s))

    def aqf_copy(block):
        return copy(actg.at[block], actg.at[block], s_aqf.at[block], r_aq.at[block], (sibling, s))

    def send_aq(i, c):
        aq_copy(dp_peer(2 * i), d).start()
        return c

    actg[d] = actq[...]
    lax.fori_loop(1, half, send_aq, 0)
    aqf_copy(d).start()

    for i in range(1, ns):
        act_copy(i, s).start()

    loads[0].wait()
    upq = jnp.concatenate([cot_all[row, mine, :] for row in range(ns)], axis=1)
    z_scr[...] = lax.dot_general(w_ref[...], upq, (((0,), (0,)), ((), ())), preferred_element_type=f32)
    zero = jnp.zeros((chans, wid), f32)
    spread = None
    for dw in (-1, 0, 1):
        total = None
        for dh in (-1, 0, 1):
            tap = 3 * (dh + 1) + dw + 1
            piece = z_scr[tap * chans : (tap + 1) * chans, :]
            if dh == 1:
                piece = jnp.concatenate([zero, piece[:, : (ns - 1) * wid]], axis=1)
            if dh == -1:
                piece = jnp.concatenate([piece[:, wid:], zero], axis=1)
            total = piece if total is None else total + piece
        total = shifted(total, -dw, wid)
        spread = total if spread is None else spread + total
    for row in range(ns):
        spread_s[row] = spread[:, row * wid : (row + 1) * wid].astype(bf16)

    def sp_copy(i, block):
        return copy(spread_s.at[strip_peer(i)], spread_r.at[block], s_sp.at[i], r_sp.at[block], (d, strip_peer(i)))

    gacc[...] = jnp.zeros_like(gacc)

    def grad_of(j):
        fill_cols(actg[j].astype(f32), qcols, wid)
        gacc[...] += lax.dot_general(
            qcols[...], cotg[j], (((1,), (1,)), ((), ())), preferred_element_type=f32
        )

    grad_of(d)

    def grad_near(i, c):
        j = dp_peer(2 * i)
        aq_copy(j, j).wait_recv()
        aqf_copy(j).start()
        cp_copy(j, j).wait_recv()
        grad_of(j)
        return c

    def grad_far(i, c):
        j = lax.rem(sibling + 2 * i, dp)
        aqf_copy(j).wait_recv()
        cp_copy(j, j).wait_recv()
        grad_of(j)
        return c

    lax.fori_loop(1, half, grad_near, 0)
    lax.fori_loop(0, half, grad_far, 0)
    gq[s] = (gacc[...].T * (1.0 / math.sqrt(dp * ns * wid))).astype(bf16)

    chunks = capp // 16

    def g_copy(i, block, c):
        src = gq.at[block, 16 * c : 16 * c + 16, :]
        return copy(src, src, s_g.at[c * ns + i], r_g.at[c * ns + block], (d, strip_peer(i)))

    for c in range(chunks):
        for i in range(1, ns):
            g_copy(i, s, c).start()
    for i in range(1, ns):
        act_copy(i, strip_peer(i)).wait_recv()
    whole = jnp.concatenate([act_all[row] for row in range(ns)], axis=1).astype(f32)
    fill_cols(whole, cols, wid)
    conv = jnp.dot(w_ref[...], cols[...], preferred_element_type=f32)
    for row in range(ns):
        conv_s[row] = conv[:, row * wid : (row + 1) * wid].astype(bf16)

    def cv_copy(i, block):
        return copy(conv_s.at[strip_peer(i)], conv_r.at[block], s_cv.at[i], r_cv.at[block], (d, strip_peer(i)))

    for load in loads[1:]:
        load.wait()

    def pub_copy(i, j, block, c):
        src = pub.at[block, 16 * c : 16 * c + 16, :]
        return copy(src, src, s_pub.at[c * dp + i], r_pub.at[c * dp + block], (j, s))

    def fw_copy(block, c):
        src = pub.at[block, 16 * c : 16 * c + 16, :]
        return copy(src, src, s_fw.at[c * dp + block], r_pub.at[c * dp + block], (sibling, s))

    for c in range(chunks):
        low, high = 16 * c, min(16 * c + 16, cap)
        for i in range(1, ns):
            g_copy(i, strip_peer(i), c).wait_recv()
        pieces = []
        for tap in range(9):
            for row in range(ns):
                pieces.append(gq[row, low : low + 16, tap * part : (tap + 1) * part])
        grads = jnp.concatenate(pieces, axis=1).astype(f32)[: high - low]
        kept = keep[low:high]
        first = first_ref[low:high, :]
        second = second_ref[low:high, :]
        master = master_ref[low:high, :]
        first_new = beta_first * first + (1.0 - beta_first) * grads
        second_new = beta_second * second + (1.0 - beta_second) * grads * grads
        update = learn_rate * (first_new / bias_first) / (jnp.sqrt(second_new / bias_second) + epsilon)
        master_new = jnp.where(kept, master - update, master)
        full = master_new
        if high - low < 16:
            full = jnp.concatenate(
                [master_new, jnp.zeros((16 - high + low, master_new.shape[1]), f32)], axis=0
            )
        pub[d, low : low + 16, :] = full.astype(bf16)

        def send_pub(i, carry, c=c):
            pub_copy(i, dp_peer(2 * i), d, c).start()
            return carry

        lax.fori_loop(1, half, send_pub, 0)
        fw_copy(d, c).start()
        nm_ref[low:high, :] = master_new
        nf_ref[low:high, :] = jnp.where(kept, first_new, first)
        nsec_ref[low:high, :] = jnp.where(kept, second_new, second)
    for i in range(1, ns):
        cv_copy(i, s).start()
        sp_copy(i, s).start()
    stores = [
        pltpu.make_async_copy(src, dst, s_out.at[k])
        for k, (src, dst) in enumerate(((nm_ref, nm_hbm), (nf_ref, nf_hbm), (nsec_ref, nsec_hbm)))
    ]
    for store in stores:
        store.start()

    slots = slot_scr[mine, :]

    def wanted(j):
        want = jnp.where(
            lax.broadcasted_iota(jnp.int32, (part, capp), 1) + j * capp == slots, 1.0, 0.0
        ).astype(bf16)
        return jnp.dot(want, pub[j], preferred_element_type=f32)

    wacc[...] = wanted(d)
    for c in range(chunks):

        def forward(i, carry, c=c):
            j = dp_peer(2 * i)
            pub_copy(i, j, j, c).wait_recv()
            fw_copy(j, c).start()
            return carry

        lax.fori_loop(1, half, forward, 0)

    def near(i, carry):
        wacc[...] += wanted(dp_peer(2 * i))
        return carry

    lax.fori_loop(1, half, near, 0)

    for i in range(1, ns):
        cv_copy(i, strip_peer(i)).wait_recv()
        sp_copy(i, strip_peer(i)).wait_recv()
    conv_r[s] = conv_s[s]
    spread_r[s] = spread_s[s]
    pix = lat_ref[0, 0].astype(f32)
    sig = 1.0 / (1.0 + jnp.exp(-pix))
    out_ref[0, 0] = (pix + conv_r[...].reshape(chans, wid).astype(f32)).astype(bf16)
    back = spread_r[0].astype(f32)
    for row in range(1, ns):
        back = back + spread_r[row].astype(f32)
    gin_ref[0, 0] = (
        cot_ref[0, 0].astype(f32) + back * (sig * (1.0 + pix * (1.0 - sig)))
    ).astype(bf16)

    def far(i, carry):
        j = lax.rem(sibling + 2 * i, dp)
        for c in range(chunks):
            fw_copy(j, c).wait_recv()
        wacc[...] += wanted(j)
        return carry

    lax.fori_loop(0, half, far, 0)
    nw_ref[...] = wacc[...].astype(bf16)

    for store in stores:
        store.wait()
    for i in range(1, ns):
        az_copy(i, s).wait_send()
        act_copy(i, s).wait_send()
        cot_copy(i, s).wait_send()
        cv_copy(i, s).wait_send()
        sp_copy(i, s).wait_send()
        for c in range(chunks):
            g_copy(i, s, c).wait_send()

    def left(i, c):
        j = dp_peer(i)
        cp_copy(j, d).wait_send()
        return c

    lax.fori_loop(1, dp, left, 0)

    def left_pub(i, c):
        for k in range(chunks):
            pub_copy(i, dp_peer(2 * i), d, k).wait_send()
            fw_copy(dp_peer(2 * i), k).wait_send()
        aq_copy(dp_peer(2 * i), d).wait_send()
        aqf_copy(dp_peer(2 * i)).wait_send()
        return c

    lax.fori_loop(1, half, left_pub, 0)
    for c in range(chunks):
        fw_copy(d, c).wait_send()
    aqf_copy(d).wait_send()


def hand_over(*refs):
    ins, outs, bufs, sem_in, sem_out = refs[:6], refs[6:12], refs[12:18], refs[18], refs[19]
    reads = [pltpu.make_async_copy(ins[k], bufs[k], sem_in.at[k]) for k in range(6)]
    writes = [pltpu.make_async_copy(bufs[k], outs[k], sem_out.at[k]) for k in range(6)]
    for c in reads:
        c.start()
    for k in range(6):
        reads[k].wait()
        writes[k].start()
    for c in writes:
        c.wait()


def local(dp, ns, latents, cotangent, weight, master, first_moment, second_moment, owner_list):
    chans, wid = latents.shape[2], latents.shape[3]
    cap = master.shape[0]
    capp = -(-cap // 16) * 16
    part = chans // ns
    chunks = capp // 16
    width = weight.shape[1]
    pixels = ns * wid
    dma = lambda n: pltpu.SemaphoreType.DMA((n,))
    vmem = pl.BlockSpec(memory_space=pltpu.VMEM)
    arrays = (latents, cotangent, weight, master, first_moment, second_moment)
    anywhere = pl.BlockSpec(memory_space=pl.ANY)
    state = [pltpu.VMEM(master.shape, f32)] * 3
    scratch = [pltpu.VMEM(weight.shape, bf16)] + state + state + [
        pltpu.VMEM((ns, part, wid), bf16),
        pltpu.VMEM((ns, chans, wid), bf16),
        pltpu.VMEM((ns, chans, wid), bf16),
        pltpu.VMEM((dp, capp, pixels), bf16),
        pltpu.VMEM((part, pixels), bf16),
        pltpu.VMEM((dp, part, pixels), bf16),
        pltpu.VMEM((dp, capp, pixels), bf16),
        pltpu.VMEM((9 * chans, pixels), bf16),
        pltpu.VMEM((9 * part, pixels), bf16),
        pltpu.VMEM((9 * chans, pixels), f32),
        pltpu.VMEM((ns, part, wid), bf16),
        pltpu.VMEM((ns, part, wid), bf16),
        pltpu.VMEM((ns, chans, wid), bf16),
        pltpu.VMEM((ns, chans, wid), bf16),
        pltpu.VMEM((ns, capp, 9 * part), bf16),
        pltpu.VMEM((9 * part, capp), f32),
        pltpu.VMEM((dp, capp, width), bf16),
        pltpu.VMEM((chans, 1), jnp.int32),
        pltpu.VMEM((part, width), f32),
    ] + [dma(n) for n in (
        ns, ns, ns, ns, dp, dp, dp, dp, ns, ns, ns, ns, ns * chunks, ns * chunks,
        dp * chunks, dp * chunks, dp * chunks, ns, ns, 4, 3, dp)]
    made = pl.pallas_call(
            functools.partial(kernel, dp, ns, cap, capp),
            out_shape=[
                jax.ShapeDtypeStruct(a.shape, a.dtype)
                for a in (latents, cotangent, weight, master, first_moment, second_moment)
            ],
            in_specs=[vmem] * 2 + [anywhere] * 4 + [vmem],
            out_specs=[vmem] * 3 + [anywhere] * 3,
            scratch_shapes=scratch,
            compiler_params=pltpu.CompilerParams(
                collective_id=0, has_side_effects=True, vmem_limit_bytes=58 * 2**20
            ),
            cost_estimate=pl.CostEstimate(flops=10**9, bytes_accessed=6 * 10**6, transcendentals=10**5),
        )(*arrays, owner_list)
    results = pl.pallas_call(
        hand_over,
        out_shape=[jax.ShapeDtypeStruct(a.shape, a.dtype) for a in arrays],
        in_specs=[anywhere] * 6,
        out_specs=[anywhere] * 6,
        scratch_shapes=[pltpu.VMEM(a.shape, a.dtype) for a in arrays] + [dma(6), dma(6)],
    )(*made)
    return tuple(results)


def solution(mesh):
    image = P("dp", "strip", None, None)
    state = P("dp", None)
    in_specs = (image, image, P("strip", None), state, state, state, P())
    out_specs = (image, image, P("strip", None), state, state, state)
    fn = functools.partial(local, mesh.shape["dp"], mesh.shape["strip"])
    return jax.shard_map(fn, mesh=mesh, in_specs=in_specs, out_specs=out_specs, check_vma=False)
```

```python
import functools
import math

import jax
import jax.numpy as jnp
from jax import lax
from jax.experimental import pallas as pl
from jax.experimental.pallas import tpu as pltpu
from jax.sharding import PartitionSpec as P

beta_first = 0.9
beta_second = 0.999
learn_rate = 0.01
epsilon = 1e-08
bias_first = 1.0 - 0.9**10
bias_second = 1.0 - 0.999**10

MESH = pl.DeviceIdType.MESH
bf16 = jnp.bfloat16
f32 = jnp.float32


def shifted(x, step, wid):
    if step == 0:
        return x
    lane = lax.broadcasted_iota(jnp.int32, x.shape, 1) % wid
    moved = pltpu.roll(x, (-step) % x.shape[1], 1)
    return jnp.where(lane == (wid - 1 if step > 0 else 0), 0.0, moved)


def fill_cols(x, out_ref, wid):
    chans, total = x.shape
    zero = jnp.zeros((chans, wid), bf16)
    for dw in (-1, 0, 1):
        moved = shifted(x, dw, wid).astype(bf16)
        padded = jnp.concatenate([zero, moved, zero], axis=1)
        for dh in (-1, 0, 1):
            tap = 3 * (dh + 1) + dw + 1
            out_ref[tap * chans : (tap + 1) * chans, :] = padded[:, (1 + dh) * wid : (1 + dh) * wid + total]


def kernel(
    dp, ns, cap, capp,
    lat_ref, cot_ref, w_hbm, master_hbm, first_hbm, second_hbm, own_ref,
    out_ref, gin_ref, nw_ref, nm_hbm, nf_hbm, nsec_hbm,
    w_ref, master_ref, first_ref, second_ref, nm_ref, nf_ref, nsec_ref, actz,
    act_all, cot_all, cotp, actg, cotg, cols, qcols, z_scr, conv_s, conv_r, spread_s, spread_r,
    gq, gacc, pub, slot_scr, wacc,
    s_act, r_act, s_cot, r_cot, s_aq, r_aq, s_cp, r_cp, s_cv, r_cv, s_sp, r_sp, s_g, r_g, s_pub, r_pub, s_fw, s_az, r_az, s_in, s_out, s_aqf,
):
    d = lax.axis_index("dp")
    s = lax.axis_index("strip")
    chans, wid = lat_ref.shape[2], lat_ref.shape[3]
    part = chans // ns
    sibling = d + 1 - 2 * lax.rem(d, 2)
    mine = pl.ds(pl.multiple_of(s * part, part), part)

    loads = [
        pltpu.make_async_copy(src, dst, s_in.at[k])
        for k, (src, dst) in enumerate(
            ((w_hbm, w_ref), (master_hbm, master_ref), (first_hbm, first_ref), (second_hbm, second_ref))
        )
    ]
    for load in loads:
        load.start()

    def copy(src, dst, ss, rs, to):
        return pltpu.make_async_remote_copy(
            src_ref=src, dst_ref=dst, send_sem=ss, recv_sem=rs, device_id=to, device_id_type=MESH
        )

    def strip_peer(i):
        return lax.rem(s + i, ns)

    def dp_peer(i):
        return lax.rem(d + i, dp)

    barrier = pltpu.get_barrier_semaphore()
    for i in range(1, ns):
        pl.semaphore_signal(barrier, inc=1, device_id=(d, strip_peer(i)), device_id_type=MESH)

    def greet(i, c):
        pl.semaphore_signal(barrier, inc=1, device_id=(dp_peer(i), s), device_id_type=MESH)
        return c

    lax.fori_loop(1, dp, greet, 0)
    pix = lat_ref[0, 0].astype(f32)
    sig = 1.0 / (1.0 + jnp.exp(-pix))
    act_all[s] = (pix * sig).astype(bf16)
    cot_all[s] = cot_ref[0, 0]
    actz[s] = act_all[s, mine, :]
    pl.semaphore_wait(barrier, ns - 1 + dp - 1)

    def act_copy(i, block):
        return copy(act_all.at[block], act_all.at[block], s_act.at[i], r_act.at[block], (d, strip_peer(i)))

    def cot_copy(i, block):
        return copy(cot_all.at[block], cot_all.at[block], s_cot.at[i], r_cot.at[block], (d, strip_peer(i)))

    def az_copy(i, block):
        rows = pl.ds(pl.multiple_of(strip_peer(i) * part, part), part)
        return copy(act_all.at[s, rows, :], actz.at[block], s_az.at[i], r_az.at[block], (d, strip_peer(i)))

    for i in range(1, ns):
        az_copy(i, s).start()
        cot_copy(i, s).start()

    orow = own_ref[...].reshape(1, chans)
    a0 = lax.broadcasted_iota(jnp.int32, (chans, chans), 0)
    a1 = lax.broadcasted_iota(jnp.int32, (chans, chans), 1)
    oc = jnp.sum(jnp.where(a0 == a1, orow.astype(f32), 0.0), axis=1, keepdims=True).astype(jnp.int32)
    same = oc == orow
    within_row = jnp.sum(jnp.where(same & (a0 < a1), 1.0, 0.0), axis=0, keepdims=True).astype(jnp.int32)
    within_col = jnp.sum(jnp.where(same & (a1 < a0), 1.0, 0.0), axis=1, keepdims=True).astype(jnp.int32)
    slot_row = orow * capp + within_row
    slot_scr[...] = oc * capp + within_col
    owned = jnp.sum(jnp.where(orow == d, 1.0, 0.0), axis=1, keepdims=True)
    keep = lax.broadcasted_iota(jnp.int32, (cap, 1), 0).astype(f32) < owned
    pick = jnp.where(
        lax.broadcasted_iota(jnp.int32, (dp * capp, chans), 0) == slot_row, 1.0, 0.0
    ).astype(bf16)

    half = dp // 2

    def cp_copy(j, block, row):
        return copy(
            cotp.at[row, j], cotg.at[block, row], s_cp.at[row * dp + j], r_cp.at[row * dp + block], (j, s)
        )

    def aq_copy(j, block, row):
        src = actg.at[block, row]
        return copy(src, src, s_aq.at[row * dp + j], r_aq.at[row * dp + block], (j, s))

    def aqf_copy(block, row):
        src = actg.at[block, row]
        at = row * dp + block
        return copy(src, src, s_aqf.at[at], r_aq.at[at], (sibling, s))

    for near_by in range(ns):
        row = strip_peer(near_by)
        if near_by:
            az_copy(near_by, row).wait_recv()
        actg[d, row] = actz[row]

        def send_aq(i, c, row=row):
            aq_copy(dp_peer(2 * i), d, row).start()
            return c

        lax.fori_loop(1, half, send_aq, 0)
        aqf_copy(d, row).start()
        if near_by:
            cot_copy(near_by, row).wait_recv()
        chosen = jnp.dot(pick, cot_all[row], preferred_element_type=f32).astype(bf16)
        cotp[row] = chosen.reshape(dp, capp, wid)

        def send_cp(i, c, row=row):
            cp_copy(dp_peer(i), d, row).start()
            return c

        lax.fori_loop(1, dp, send_cp, 0)
        cotg[d, row] = cotp[row, d]

    for i in range(1, ns):
        act_copy(i, s).start()

    loads[0].wait()
    upq = jnp.concatenate([cot_all[row, mine, :] for row in range(ns)], axis=1)
    z_scr[...] = lax.dot_general(w_ref[...], upq, (((0,), (0,)), ((), ())), preferred_element_type=f32)
    zero = jnp.zeros((chans, wid), f32)
    spread = None
    for dw in (-1, 0, 1):
        total = None
        for dh in (-1, 0, 1):
            tap = 3 * (dh + 1) + dw + 1
            piece = z_scr[tap * chans : (tap + 1) * chans, :]
            if dh == 1:
                piece = jnp.concatenate([zero, piece[:, : (ns - 1) * wid]], axis=1)
            if dh == -1:
                piece = jnp.concatenate([piece[:, wid:], zero], axis=1)
            total = piece if total is None else total + piece
        total = shifted(total, -dw, wid)
        spread = total if spread is None else spread + total
    for row in range(ns):
        spread_s[row] = spread[:, row * wid : (row + 1) * wid].astype(bf16)

    def sp_copy(i, block):
        return copy(spread_s.at[strip_peer(i)], spread_r.at[block], s_sp.at[i], r_sp.at[block], (d, strip_peer(i)))

    gacc[...] = jnp.zeros_like(gacc)

    def grad_of(j):
        fill_cols(jnp.concatenate([actg[j, row] for row in range(ns)], axis=1).astype(f32), qcols, wid)
        rows = jnp.concatenate([cotg[j, row] for row in range(ns)], axis=1)
        gacc[...] += lax.dot_general(
            qcols[...], rows, (((1,), (1,)), ((), ())), preferred_element_type=f32
        )

    grad_of(d)

    def grad_near(i, c):
        j = dp_peer(2 * i)
        for row in range(ns):
            aq_copy(j, j, row).wait_recv()
            aqf_copy(j, row).start()
        for row in range(ns):
            cp_copy(j, j, row).wait_recv()
        grad_of(j)
        return c

    def grad_far(i, c):
        j = lax.rem(sibling + 2 * i, dp)
        for row in range(ns):
            aqf_copy(j, row).wait_recv()
            cp_copy(j, j, row).wait_recv()
        grad_of(j)
        return c

    lax.fori_loop(1, half, grad_near, 0)
    lax.fori_loop(0, half, grad_far, 0)
    gq[s] = (gacc[...].T * (1.0 / math.sqrt(dp * ns * wid))).astype(bf16)

    chunks = capp // 16

    def g_copy(i, block, c):
        src = gq.at[block, 16 * c : 16 * c + 16, :]
        return copy(src, src, s_g.at[c * ns + i], r_g.at[c * ns + block], (d, strip_peer(i)))

    for c in range(chunks):
        for i in range(1, ns):
            g_copy(i, s, c).start()
    for i in range(1, ns):
        act_copy(i, strip_peer(i)).wait_recv()
    whole = jnp.concatenate([act_all[row] for row in range(ns)], axis=1).astype(f32)
    fill_cols(whole, cols, wid)
    conv = jnp.dot(w_ref[...], cols[...], preferred_element_type=f32)
    for row in range(ns):
        conv_s[row] = conv[:, row * wid : (row + 1) * wid].astype(bf16)

    def cv_copy(i, block):
        return copy(conv_s.at[strip_peer(i)], conv_r.at[block], s_cv.at[i], r_cv.at[block], (d, strip_peer(i)))

    for load in loads[1:]:
        load.wait()

    def pub_copy(i, j, block, c):
        src = pub.at[block, 16 * c : 16 * c + 16, :]
        return copy(src, src, s_pub.at[c * dp + i], r_pub.at[c * dp + block], (j, s))

    def fw_copy(block, c):
        src = pub.at[block, 16 * c : 16 * c + 16, :]
        return copy(src, src, s_fw.at[c * dp + block], r_pub.at[c * dp + block], (sibling, s))

    for c in range(chunks):
        low, high = 16 * c, min(16 * c + 16, cap)
        for i in range(1, ns):
            g_copy(i, strip_peer(i), c).wait_recv()
        pieces = []
        for tap in range(9):
            for row in range(ns):
                pieces.append(gq[row, low : low + 16, tap * part : (tap + 1) * part])
        grads = jnp.concatenate(pieces, axis=1).astype(f32)[: high - low]
        kept = keep[low:high]
        first = first_ref[low:high, :]
        second = second_ref[low:high, :]
        master = master_ref[low:high, :]
        first_new = beta_first * first + (1.0 - beta_first) * grads
        second_new = beta_second * second + (1.0 - beta_second) * grads * grads
        update = learn_rate * (first_new / bias_first) / (jnp.sqrt(second_new / bias_second) + epsilon)
        master_new = jnp.where(kept, master - update, master)
        full = master_new
        if high - low < 16:
            full = jnp.concatenate(
                [master_new, jnp.zeros((16 - high + low, master_new.shape[1]), f32)], axis=0
            )
        pub[d, low : low + 16, :] = full.astype(bf16)

        def send_pub(i, carry, c=c):
            pub_copy(i, dp_peer(2 * i), d, c).start()
            return carry

        lax.fori_loop(1, half, send_pub, 0)
        fw_copy(d, c).start()
        nm_ref[low:high, :] = master_new
        nf_ref[low:high, :] = jnp.where(kept, first_new, first)
        nsec_ref[low:high, :] = jnp.where(kept, second_new, second)
    for i in range(1, ns):
        cv_copy(i, s).start()
        sp_copy(i, s).start()
    stores = [
        pltpu.make_async_copy(src, dst, s_out.at[k])
        for k, (src, dst) in enumerate(((nm_ref, nm_hbm), (nf_ref, nf_hbm), (nsec_ref, nsec_hbm)))
    ]
    for store in stores:
        store.start()

    slots = slot_scr[mine, :]

    def wanted(j):
        want = jnp.where(
            lax.broadcasted_iota(jnp.int32, (part, capp), 1) + j * capp == slots, 1.0, 0.0
        ).astype(bf16)
        return jnp.dot(want, pub[j], preferred_element_type=f32)

    wacc[...] = wanted(d)
    for c in range(chunks):

        def forward(i, carry, c=c):
            j = dp_peer(2 * i)
            pub_copy(i, j, j, c).wait_recv()
            fw_copy(j, c).start()
            return carry

        lax.fori_loop(1, half, forward, 0)

    def near(i, carry):
        wacc[...] += wanted(dp_peer(2 * i))
        return carry

    lax.fori_loop(1, half, near, 0)

    for i in range(1, ns):
        cv_copy(i, strip_peer(i)).wait_recv()
        sp_copy(i, strip_peer(i)).wait_recv()
    conv_r[s] = conv_s[s]
    spread_r[s] = spread_s[s]
    pix = lat_ref[0, 0].astype(f32)
    sig = 1.0 / (1.0 + jnp.exp(-pix))
    out_ref[0, 0] = (pix + conv_r[...].reshape(chans, wid).astype(f32)).astype(bf16)
    back = spread_r[0].astype(f32)
    for row in range(1, ns):
        back = back + spread_r[row].astype(f32)
    gin_ref[0, 0] = (
        cot_ref[0, 0].astype(f32) + back * (sig * (1.0 + pix * (1.0 - sig)))
    ).astype(bf16)

    def far(i, carry):
        j = lax.rem(sibling + 2 * i, dp)
        for c in range(chunks):
            fw_copy(j, c).wait_recv()
        wacc[...] += wanted(j)
        return carry

    lax.fori_loop(0, half, far, 0)
    nw_ref[...] = wacc[...].astype(bf16)

    for store in stores:
        store.wait()
    for i in range(1, ns):
        az_copy(i, s).wait_send()
        act_copy(i, s).wait_send()
        cot_copy(i, s).wait_send()
        cv_copy(i, s).wait_send()
        sp_copy(i, s).wait_send()
        for c in range(chunks):
            g_copy(i, s, c).wait_send()

    def left(i, c):
        j = dp_peer(i)
        for row in range(ns):
            cp_copy(j, d, row).wait_send()
        return c

    lax.fori_loop(1, dp, left, 0)

    def left_pub(i, c):
        for k in range(chunks):
            pub_copy(i, dp_peer(2 * i), d, k).wait_send()
            fw_copy(dp_peer(2 * i), k).wait_send()
        for row in range(ns):
            aq_copy(dp_peer(2 * i), d, row).wait_send()
            aqf_copy(dp_peer(2 * i), row).wait_send()
        return c

    lax.fori_loop(1, half, left_pub, 0)
    for c in range(chunks):
        fw_copy(d, c).wait_send()
    for row in range(ns):
        aqf_copy(d, row).wait_send()


def hand_over(*refs):
    ins, outs, bufs, sem_in, sem_out = refs[:6], refs[6:12], refs[12:18], refs[18], refs[19]
    reads = [pltpu.make_async_copy(ins[k], bufs[k], sem_in.at[k]) for k in range(6)]
    writes = [pltpu.make_async_copy(bufs[k], outs[k], sem_out.at[k]) for k in range(6)]
    for c in reads:
        c.start()
    for k in range(6):
        reads[k].wait()
        writes[k].start()
    for c in writes:
        c.wait()


def local(dp, ns, latents, cotangent, weight, master, first_moment, second_moment, owner_list):
    chans, wid = latents.shape[2], latents.shape[3]
    cap = master.shape[0]
    capp = -(-cap // 16) * 16
    part = chans // ns
    chunks = capp // 16
    width = weight.shape[1]
    pixels = ns * wid
    dma = lambda n: pltpu.SemaphoreType.DMA((n,))
    vmem = pl.BlockSpec(memory_space=pltpu.VMEM)
    arrays = (latents, cotangent, weight, master, first_moment, second_moment)
    anywhere = pl.BlockSpec(memory_space=pl.ANY)
    state = [pltpu.VMEM(master.shape, f32)] * 3
    scratch = [pltpu.VMEM(weight.shape, bf16)] + state + state + [
        pltpu.VMEM((ns, part, wid), bf16),
        pltpu.VMEM((ns, chans, wid), bf16),
        pltpu.VMEM((ns, chans, wid), bf16),
        pltpu.VMEM((ns, dp, capp, wid), bf16),
        pltpu.VMEM((dp, ns, part, wid), bf16),
        pltpu.VMEM((dp, ns, capp, wid), bf16),
        pltpu.VMEM((9 * chans, pixels), bf16),
        pltpu.VMEM((9 * part, pixels), bf16),
        pltpu.VMEM((9 * chans, pixels), f32),
        pltpu.VMEM((ns, part, wid), bf16),
        pltpu.VMEM((ns, part, wid), bf16),
        pltpu.VMEM((ns, chans, wid), bf16),
        pltpu.VMEM((ns, chans, wid), bf16),
        pltpu.VMEM((ns, capp, 9 * part), bf16),
        pltpu.VMEM((9 * part, capp), f32),
        pltpu.VMEM((dp, capp, width), bf16),
        pltpu.VMEM((chans, 1), jnp.int32),
        pltpu.VMEM((part, width), f32),
    ] + [dma(n) for n in (
        ns, ns, ns, ns, ns * dp, ns * dp, ns * dp, ns * dp, ns, ns, ns, ns, ns * chunks, ns * chunks,
        dp * chunks, dp * chunks, dp * chunks, ns, ns, 4, 3, ns * dp)]
    made = pl.pallas_call(
            functools.partial(kernel, dp, ns, cap, capp),
            out_shape=[
                jax.ShapeDtypeStruct(a.shape, a.dtype)
                for a in (latents, cotangent, weight, master, first_moment, second_moment)
            ],
            in_specs=[vmem] * 2 + [anywhere] * 4 + [vmem],
            out_specs=[vmem] * 3 + [anywhere] * 3,
            scratch_shapes=scratch,
            compiler_params=pltpu.CompilerParams(
                collective_id=0, has_side_effects=True, vmem_limit_bytes=58 * 2**20
            ),
            cost_estimate=pl.CostEstimate(flops=10**9, bytes_accessed=6 * 10**6, transcendentals=10**5),
        )(*arrays, owner_list)
    results = pl.pallas_call(
        hand_over,
        out_shape=[jax.ShapeDtypeStruct(a.shape, a.dtype) for a in arrays],
        in_specs=[anywhere] * 6,
        out_specs=[anywhere] * 6,
        scratch_shapes=[pltpu.VMEM(a.shape, a.dtype) for a in arrays] + [dma(6), dma(6)],
    )(*made)
    return tuple(results)


def solution(mesh):
    image = P("dp", "strip", None, None)
    state = P("dp", None)
    in_specs = (image, image, P("strip", None), state, state, state, P())
    out_specs = (image, image, P("strip", None), state, state, state)
    fn = functools.partial(local, mesh.shape["dp"], mesh.shape["strip"])
    return jax.shard_map(fn, mesh=mesh, in_specs=in_specs, out_specs=out_specs, check_vma=False)
```

```python
import functools
import math

import jax
import jax.numpy as jnp
from jax import lax
from jax.experimental import pallas as pl
from jax.experimental.pallas import tpu as pltpu
from jax.sharding import PartitionSpec as P

beta_first = 0.9
beta_second = 0.999
learn_rate = 0.01
epsilon = 1e-08
bias_first = 1.0 - 0.9**10
bias_second = 1.0 - 0.999**10

MESH = pl.DeviceIdType.MESH
bf16 = jnp.bfloat16
f32 = jnp.float32


def shifted(x, step, wid):
    if step == 0:
        return x
    lane = lax.broadcasted_iota(jnp.int32, x.shape, 1) % wid
    moved = pltpu.roll(x, (-step) % x.shape[1], 1)
    return jnp.where(lane == (wid - 1 if step > 0 else 0), 0.0, moved)


def fill_cols(x, out_ref, wid):
    chans, total = x.shape
    zero = jnp.zeros((chans, wid), bf16)
    for dw in (-1, 0, 1):
        moved = shifted(x, dw, wid).astype(bf16)
        padded = jnp.concatenate([zero, moved, zero], axis=1)
        for dh in (-1, 0, 1):
            tap = 3 * (dh + 1) + dw + 1
            out_ref[tap * chans : (tap + 1) * chans, :] = padded[:, (1 + dh) * wid : (1 + dh) * wid + total]


def kernel(
    dp, ns, cap, capp,
    lat_ref, cot_ref, w_hbm, master_hbm, first_hbm, second_hbm, own_ref,
    out_ref, gin_ref, nw_ref, nm_hbm, nf_hbm, nsec_hbm,
    w_ref, master_ref, first_ref, second_ref, nm_ref, nf_ref, nsec_ref, actz,
    act_all, cot_all, cotp, actg, cotg, cols, qcols, z_scr, conv_s, conv_r, spread_s, spread_r,
    gq, gacc, pub, slot_scr, wacc,
    s_act, r_act, s_cot, r_cot, s_aq, r_aq, s_cp, r_cp, s_cv, r_cv, s_sp, r_sp, s_g, r_g, s_pub, r_pub, s_fw, s_az, r_az, s_in, s_out, s_aqf,
):
    d = lax.axis_index("dp")
    s = lax.axis_index("strip")
    chans, wid = lat_ref.shape[2], lat_ref.shape[3]
    part = chans // ns
    sibling = d + 1 - 2 * lax.rem(d, 2)
    mine = pl.ds(pl.multiple_of(s * part, part), part)

    loads = [
        pltpu.make_async_copy(src, dst, s_in.at[k])
        for k, (src, dst) in enumerate(
            ((w_hbm, w_ref), (master_hbm, master_ref), (first_hbm, first_ref), (second_hbm, second_ref))
        )
    ]
    for load in loads:
        load.start()

    def copy(src, dst, ss, rs, to):
        return pltpu.make_async_remote_copy(
            src_ref=src, dst_ref=dst, send_sem=ss, recv_sem=rs, device_id=to, device_id_type=MESH
        )

    def strip_peer(i):
        return lax.rem(s + i, ns)

    def dp_peer(i):
        return lax.rem(d + i, dp)

    barrier = pltpu.get_barrier_semaphore()
    for i in range(1, ns):
        pl.semaphore_signal(barrier, inc=1, device_id=(d, strip_peer(i)), device_id_type=MESH)

    def greet(i, c):
        pl.semaphore_signal(barrier, inc=1, device_id=(dp_peer(i), s), device_id_type=MESH)
        return c

    lax.fori_loop(1, dp, greet, 0)
    pix = lat_ref[0, 0].astype(f32)
    sig = 1.0 / (1.0 + jnp.exp(-pix))
    act_all[s] = (pix * sig).astype(bf16)
    cot_all[s] = cot_ref[0, 0]
    actz[s] = act_all[s, mine, :]
    pl.semaphore_wait(barrier, ns - 1 + dp - 1)

    def act_copy(i, block):
        return copy(act_all.at[block], act_all.at[block], s_act.at[i], r_act.at[block], (d, strip_peer(i)))

    def cot_copy(i, block):
        return copy(cot_all.at[block], cot_all.at[block], s_cot.at[i], r_cot.at[block], (d, strip_peer(i)))

    def az_copy(i, block):
        rows = pl.ds(pl.multiple_of(strip_peer(i) * part, part), part)
        return copy(act_all.at[s, rows, :], actz.at[block], s_az.at[i], r_az.at[block], (d, strip_peer(i)))

    for i in range(1, ns):
        az_copy(i, s).start()
        cot_copy(i, s).start()

    orow = own_ref[...].reshape(1, chans)
    a0 = lax.broadcasted_iota(jnp.int32, (chans, chans), 0)
    a1 = lax.broadcasted_iota(jnp.int32, (chans, chans), 1)
    oc = jnp.sum(jnp.where(a0 == a1, orow.astype(f32), 0.0), axis=1, keepdims=True).astype(jnp.int32)
    same = oc == orow
    within_row = jnp.sum(jnp.where(same & (a0 < a1), 1.0, 0.0), axis=0, keepdims=True).astype(jnp.int32)
    within_col = jnp.sum(jnp.where(same & (a1 < a0), 1.0, 0.0), axis=1, keepdims=True).astype(jnp.int32)
    slot_row = orow * capp + within_row
    slot_scr[...] = oc * capp + within_col
    owned = jnp.sum(jnp.where(orow == d, 1.0, 0.0), axis=1, keepdims=True)
    keep = lax.broadcasted_iota(jnp.int32, (cap, 1), 0).astype(f32) < owned
    pick = jnp.where(
        lax.broadcasted_iota(jnp.int32, (dp * capp, chans), 0) == slot_row, 1.0, 0.0
    ).astype(bf16)

    half = dp // 2

    def cp_copy(j, block, row):
        return copy(
            cotp.at[row, j], cotg.at[block, row], s_cp.at[row * dp + j], r_cp.at[row * dp + block], (j, s)
        )

    def aq_copy(j, block, row):
        src = actg.at[block, row]
        return copy(src, src, s_aq.at[row * dp + j], r_aq.at[row * dp + block], (j, s))

    def aqf_copy(block, row):
        src = actg.at[block, row]
        at = row * dp + block
        return copy(src, src, s_aqf.at[at], r_aq.at[at], (sibling, s))

    for near_by in range(ns):
        row = strip_peer(near_by)
        if near_by:
            az_copy(near_by, row).wait_recv()
        actg[d, row] = actz[row]

        def send_aq(i, c, row=row):
            aq_copy(dp_peer(2 * i), d, row).start()
            return c

        lax.fori_loop(1, half, send_aq, 0)
        aqf_copy(d, row).start()
        if near_by:
            cot_copy(near_by, row).wait_recv()
        chosen = jnp.dot(pick, cot_all[row], preferred_element_type=f32).astype(bf16)
        cotp[row] = chosen.reshape(dp, capp, wid)

        def send_cp(i, c, row=row):
            cp_copy(dp_peer(i), d, row).start()
            return c

        lax.fori_loop(1, dp, send_cp, 0)
        cotg[d, row] = cotp[row, d]

    for i in range(1, ns):
        act_copy(i, s).start()

    loads[0].wait()
    upq = jnp.concatenate([cot_all[row, mine, :] for row in range(ns)], axis=1)
    z_scr[...] = lax.dot_general(w_ref[...], upq, (((0,), (0,)), ((), ())), preferred_element_type=f32)
    zero = jnp.zeros((chans, wid), f32)
    spread = None
    for dw in (-1, 0, 1):
        total = None
        for dh in (-1, 0, 1):
            tap = 3 * (dh + 1) + dw + 1
            piece = z_scr[tap * chans : (tap + 1) * chans, :]
            if dh == 1:
                piece = jnp.concatenate([zero, piece[:, : (ns - 1) * wid]], axis=1)
            if dh == -1:
                piece = jnp.concatenate([piece[:, wid:], zero], axis=1)
            total = piece if total is None else total + piece
        total = shifted(total, -dw, wid)
        spread = total if spread is None else spread + total
    for row in range(ns):
        spread_s[row] = spread[:, row * wid : (row + 1) * wid].astype(bf16)

    def sp_copy(i, block):
        return copy(spread_s.at[strip_peer(i)], spread_r.at[block], s_sp.at[i], r_sp.at[block], (d, strip_peer(i)))

    gacc[...] = jnp.zeros_like(gacc)

    def grad_of(j):
        fill_cols(jnp.concatenate([actg[j, row] for row in range(ns)], axis=1).astype(f32), qcols, wid)
        rows = jnp.concatenate([cotg[j, row] for row in range(ns)], axis=1)
        gacc[...] += lax.dot_general(
            qcols[...], rows, (((1,), (1,)), ((), ())), preferred_element_type=f32
        )

    grad_of(d)

    def grad_near(i, c):
        j = dp_peer(2 * i)
        for row in range(ns):
            aq_copy(j, j, row).wait_recv()
            aqf_copy(j, row).start()
        for row in range(ns):
            cp_copy(j, j, row).wait_recv()
        grad_of(j)
        return c

    def grad_far(i, c):
        j = lax.rem(sibling + 2 * i, dp)
        for row in range(ns):
            aqf_copy(j, row).wait_recv()
            cp_copy(j, j, row).wait_recv()
        grad_of(j)
        return c

    lax.fori_loop(1, half, grad_near, 0)
    lax.fori_loop(0, half, grad_far, 0)
    gq[s] = (gacc[...].T * (1.0 / math.sqrt(dp * ns * wid))).astype(bf16)

    chunks = capp // 16

    def g_copy(i, block, c):
        src = gq.at[block, 16 * c : 16 * c + 16, :]
        return copy(src, src, s_g.at[c * ns + i], r_g.at[c * ns + block], (d, strip_peer(i)))

    for c in range(chunks):
        for i in range(1, ns):
            g_copy(i, s, c).start()
    for load in loads[1:]:
        load.wait()

    def pub_copy(i, j, block, c):
        src = pub.at[block, 16 * c : 16 * c + 16, :]
        return copy(src, src, s_pub.at[c * dp + i], r_pub.at[c * dp + block], (j, s))

    def fw_copy(block, c):
        src = pub.at[block, 16 * c : 16 * c + 16, :]
        return copy(src, src, s_fw.at[c * dp + block], r_pub.at[c * dp + block], (sibling, s))

    for c in range(chunks):
        low, high = 16 * c, min(16 * c + 16, cap)
        for i in range(1, ns):
            g_copy(i, strip_peer(i), c).wait_recv()
        pieces = []
        for tap in range(9):
            for row in range(ns):
                pieces.append(gq[row, low : low + 16, tap * part : (tap + 1) * part])
        grads = jnp.concatenate(pieces, axis=1).astype(f32)[: high - low]
        kept = keep[low:high]
        first = first_ref[low:high, :]
        second = second_ref[low:high, :]
        master = master_ref[low:high, :]
        first_new = beta_first * first + (1.0 - beta_first) * grads
        second_new = beta_second * second + (1.0 - beta_second) * grads * grads
        update = learn_rate * (first_new / bias_first) / (jnp.sqrt(second_new / bias_second) + epsilon)
        master_new = jnp.where(kept, master - update, master)
        full = master_new
        if high - low < 16:
            full = jnp.concatenate(
                [master_new, jnp.zeros((16 - high + low, master_new.shape[1]), f32)], axis=0
            )
        pub[d, low : low + 16, :] = full.astype(bf16)

        def send_pub(i, carry, c=c):
            pub_copy(i, dp_peer(2 * i), d, c).start()
            return carry

        lax.fori_loop(1, half, send_pub, 0)
        fw_copy(d, c).start()
        nm_ref[low:high, :] = master_new
        nf_ref[low:high, :] = jnp.where(kept, first_new, first)
        nsec_ref[low:high, :] = jnp.where(kept, second_new, second)
    for i in range(1, ns):
        sp_copy(i, s).start()
    for i in range(1, ns):
        act_copy(i, strip_peer(i)).wait_recv()
    whole = jnp.concatenate([act_all[row] for row in range(ns)], axis=1).astype(f32)
    fill_cols(whole, cols, wid)
    conv = jnp.dot(w_ref[...], cols[...], preferred_element_type=f32)
    for row in range(ns):
        conv_s[row] = conv[:, row * wid : (row + 1) * wid].astype(bf16)

    def cv_copy(i, block):
        return copy(conv_s.at[strip_peer(i)], conv_r.at[block], s_cv.at[i], r_cv.at[block], (d, strip_peer(i)))

    for i in range(1, ns):
        cv_copy(i, s).start()
    stores = [
        pltpu.make_async_copy(src, dst, s_out.at[k])
        for k, (src, dst) in enumerate(((nm_ref, nm_hbm), (nf_ref, nf_hbm), (nsec_ref, nsec_hbm)))
    ]
    for store in stores:
        store.start()

    slots = slot_scr[mine, :]

    def wanted(j):
        want = jnp.where(
            lax.broadcasted_iota(jnp.int32, (part, capp), 1) + j * capp == slots, 1.0, 0.0
        ).astype(bf16)
        return jnp.dot(want, pub[j], preferred_element_type=f32)

    wacc[...] = wanted(d)
    for c in range(chunks):

        def forward(i, carry, c=c):
            j = dp_peer(2 * i)
            pub_copy(i, j, j, c).wait_recv()
            fw_copy(j, c).start()
            return carry

        lax.fori_loop(1, half, forward, 0)

    def near(i, carry):
        wacc[...] += wanted(dp_peer(2 * i))
        return carry

    lax.fori_loop(1, half, near, 0)

    for i in range(1, ns):
        cv_copy(i, strip_peer(i)).wait_recv()
        sp_copy(i, strip_peer(i)).wait_recv()
    conv_r[s] = conv_s[s]
    spread_r[s] = spread_s[s]
    pix = lat_ref[0, 0].astype(f32)
    sig = 1.0 / (1.0 + jnp.exp(-pix))
    out_ref[0, 0] = (pix + conv_r[...].reshape(chans, wid).astype(f32)).astype(bf16)
    back = spread_r[0].astype(f32)
    for row in range(1, ns):
        back = back + spread_r[row].astype(f32)
    gin_ref[0, 0] = (
        cot_ref[0, 0].astype(f32) + back * (sig * (1.0 + pix * (1.0 - sig)))
    ).astype(bf16)

    def far(i, carry):
        j = lax.rem(sibling + 2 * i, dp)
        for c in range(chunks):
            fw_copy(j, c).wait_recv()
        wacc[...] += wanted(j)
        return carry

    lax.fori_loop(0, half, far, 0)
    nw_ref[...] = wacc[...].astype(bf16)

    for store in stores:
        store.wait()
    for i in range(1, ns):
        az_copy(i, s).wait_send()
        act_copy(i, s).wait_send()
        cot_copy(i, s).wait_send()
        cv_copy(i, s).wait_send()
        sp_copy(i, s).wait_send()
        for c in range(chunks):
            g_copy(i, s, c).wait_send()

    def left(i, c):
        j = dp_peer(i)
        for row in range(ns):
            cp_copy(j, d, row).wait_send()
        return c

    lax.fori_loop(1, dp, left, 0)

    def left_pub(i, c):
        for k in range(chunks):
            pub_copy(i, dp_peer(2 * i), d, k).wait_send()
            fw_copy(dp_peer(2 * i), k).wait_send()
        for row in range(ns):
            aq_copy(dp_peer(2 * i), d, row).wait_send()
            aqf_copy(dp_peer(2 * i), row).wait_send()
        return c

    lax.fori_loop(1, half, left_pub, 0)
    for c in range(chunks):
        fw_copy(d, c).wait_send()
    for row in range(ns):
        aqf_copy(d, row).wait_send()


def hand_over(*refs):
    ins, outs, bufs, sem_in, sem_out = refs[:6], refs[6:12], refs[12:18], refs[18], refs[19]
    reads = [pltpu.make_async_copy(ins[k], bufs[k], sem_in.at[k]) for k in range(6)]
    writes = [pltpu.make_async_copy(bufs[k], outs[k], sem_out.at[k]) for k in range(6)]
    for c in reads:
        c.start()
    for k in range(6):
        reads[k].wait()
        writes[k].start()
    for c in writes:
        c.wait()


def local(dp, ns, latents, cotangent, weight, master, first_moment, second_moment, owner_list):
    chans, wid = latents.shape[2], latents.shape[3]
    cap = master.shape[0]
    capp = -(-cap // 16) * 16
    part = chans // ns
    chunks = capp // 16
    width = weight.shape[1]
    pixels = ns * wid
    dma = lambda n: pltpu.SemaphoreType.DMA((n,))
    vmem = pl.BlockSpec(memory_space=pltpu.VMEM)
    arrays = (latents, cotangent, weight, master, first_moment, second_moment)
    anywhere = pl.BlockSpec(memory_space=pl.ANY)
    state = [pltpu.VMEM(master.shape, f32)] * 3
    scratch = [pltpu.VMEM(weight.shape, bf16)] + state + state + [
        pltpu.VMEM((ns, part, wid), bf16),
        pltpu.VMEM((ns, chans, wid), bf16),
        pltpu.VMEM((ns, chans, wid), bf16),
        pltpu.VMEM((ns, dp, capp, wid), bf16),
        pltpu.VMEM((dp, ns, part, wid), bf16),
        pltpu.VMEM((dp, ns, capp, wid), bf16),
        pltpu.VMEM((9 * chans, pixels), bf16),
        pltpu.VMEM((9 * part, pixels), bf16),
        pltpu.VMEM((9 * chans, pixels), f32),
        pltpu.VMEM((ns, part, wid), bf16),
        pltpu.VMEM((ns, part, wid), bf16),
        pltpu.VMEM((ns, chans, wid), bf16),
        pltpu.VMEM((ns, chans, wid), bf16),
        pltpu.VMEM((ns, capp, 9 * part), bf16),
        pltpu.VMEM((9 * part, capp), f32),
        pltpu.VMEM((dp, capp, width), bf16),
        pltpu.VMEM((chans, 1), jnp.int32),
        pltpu.VMEM((part, width), f32),
    ] + [dma(n) for n in (
        ns, ns, ns, ns, ns * dp, ns * dp, ns * dp, ns * dp, ns, ns, ns, ns, ns * chunks, ns * chunks,
        dp * chunks, dp * chunks, dp * chunks, ns, ns, 4, 3, ns * dp)]
    made = pl.pallas_call(
            functools.partial(kernel, dp, ns, cap, capp),
            out_shape=[
                jax.ShapeDtypeStruct(a.shape, a.dtype)
                for a in (latents, cotangent, weight, master, first_moment, second_moment)
            ],
            in_specs=[vmem] * 2 + [anywhere] * 4 + [vmem],
            out_specs=[vmem] * 3 + [anywhere] * 3,
            scratch_shapes=scratch,
            compiler_params=pltpu.CompilerParams(
                collective_id=0, has_side_effects=True, vmem_limit_bytes=58 * 2**20
            ),
            cost_estimate=pl.CostEstimate(flops=10**9, bytes_accessed=6 * 10**6, transcendentals=10**5),
        )(*arrays, owner_list)
    results = pl.pallas_call(
        hand_over,
        out_shape=[jax.ShapeDtypeStruct(a.shape, a.dtype) for a in arrays],
        in_specs=[anywhere] * 6,
        out_specs=[anywhere] * 6,
        scratch_shapes=[pltpu.VMEM(a.shape, a.dtype) for a in arrays] + [dma(6), dma(6)],
    )(*made)
    return tuple(results)


def solution(mesh):
    image = P("dp", "strip", None, None)
    state = P("dp", None)
    in_specs = (image, image, P("strip", None), state, state, state, P())
    out_specs = (image, image, P("strip", None), state, state, state)
    fn = functools.partial(local, mesh.shape["dp"], mesh.shape["strip"])
    return jax.shard_map(fn, mesh=mesh, in_specs=in_specs, out_specs=out_specs, check_vma=False)
```
